32 devices in a mesh: domain: 8 (over y, x, core), band: 4 (over z).
Axes of the slice: x: 2, y: 2, z: 4, core: 2. Of those that a mesh axis runs over, the one named last changes fastest.
Arguments:
- orbitals: float32 [512, 72, 1152], P('band', 'domain'), may hold values from -6 to 6
- potential: float32 [72, 1152], P('domain'), may hold values from -16 to 4
Outputs:
- filtered: float32 [512, 72, 1152], P('band', 'domain')
- proj_ham: float32 [512, 512], P('domain', 'band')
- proj_intersection: float32 [512, 512], P('domain', 'band')
The draws below stay inside these ranges and needn't reach their ends.
All inputs are finite; a program needn't handle non-finite values.
Results may differ from the reference program's by a relative error of at most 0.0003.
Values may be sent and summed in bfloat16 or wider, within the bound.
No kernel may reach another device: no remote copies, remote signals or barrier semaphores. Data moves between devices by JAX's collectives and lax.ppermute only.
A program may use at most 128 MiB of HBM per device.

```python
import math
import jax
import jax.numpy as jnp
from jax import lax

ORB = 512
CX = 9
NY = 8
NZ = 144
NX = 72
NCELLS = 82944
N_DOMAIN = 8


def draw_orbitals(key, part):
    key = jax.random.fold_in(key, 11)
    keys = jax.random.split(key, 6)
    block = ORB // N_DOMAIN
    xpos = jnp.arange(NX, dtype=jnp.int32)
    alternate = jnp.where(xpos % 2 == 0, 1.0, -1.0).astype(jnp.float32)
    ypos = jnp.arange(NY, dtype=jnp.float32)
    zpos = jnp.arange(NZ, dtype=jnp.float32)
    wave_y = jax.random.randint(keys[0], (ORB,), 1, 3).astype(jnp.float32)
    wave_z = jax.random.randint(keys[1], (ORB,), 1, 3).astype(jnp.float32)
    phase = jax.random.uniform(keys[2], (ORB,), jnp.float32, -math.pi, math.pi)
    angle_y = 2.0 * math.pi * wave_y[:, None, None] * ypos[None, :, None] / NY
    angle_z = 2.0 * math.pi * wave_z[:, None, None] * zpos[None, None, :] / NZ
    envelope = jnp.cos(angle_y + angle_z + phase[:, None, None]).reshape(ORB, NY * NZ)
    owner = jax.random.permutation(keys[3], N_DOMAIN)
    row_owner = owner[jnp.arange(ORB, dtype=jnp.int32) // block]
    slab = xpos // CX
    spike = jnp.where(row_owner[:, None] == slab[None, :], 2.0, 1.0).astype(jnp.float32)
    amplitude = jnp.full((ORB,), 1.5, jnp.float32)
    rough = 1.0 + 0.3 * jnp.clip(jax.random.normal(keys[5], (ORB, NX, NY * NZ), jnp.float32), -2.0, 2.0)
    values = amplitude[:, None, None] * spike[:, :, None] * alternate[None, :, None] * envelope[:, None, :] * rough
    return jnp.clip(values, -6.0, 6.0).astype(jnp.float32)


def steps_of(rng, shape, cuts, smallest, top_value):
    def one(dim, blocks):
        heights = jax.random.uniform(jax.random.fold_in(jax.random.fold_in(rng, 6), dim), (blocks,), jnp.float32, smallest / len(cuts), top_value / len(cuts))
        return jnp.repeat(jnp.exp(heights), shape[dim] // blocks).reshape((-1,) + (1,) * (len(shape) - dim - 1))

    level = one(*cuts[0])
    for cut in cuts[1:]:
        level = level * one(*cut)
    return level


def setup_inputs(seed: int = 0) -> dict:
    key_list = jax.random.split(jax.random.key(seed), 3)
    orbitals = draw_orbitals(jax.random.fold_in(key_list[2], 71), 0)
    potential = jnp.clip(-16.0 + 20.0 * jax.random.uniform(key_list[1], (NX, NY * NZ), jnp.float32) ** steps_of(key_list[1], (NX, NY * NZ), ((0, 8),), -0.2, 0.2), -16.0, 4.0)
    return {"orbitals": orbitals, "potential": potential}


coeffs = (-205.0 / 72.0, 8.0 / 5.0, -1.0 / 5.0, 8.0 / 315.0, -1.0 / 560.0)
kinetic = -0.5 / 0.09
center = 68.0
half_width = 48.0


def second_diff(padded, axis, length):
    total = coeffs[0] * lax.slice_in_dim(padded, 4, 4 + length, axis=axis)
    for shift_k in range(1, 5):
        upper = lax.slice_in_dim(padded, 4 + shift_k, 4 + shift_k + length, axis=axis)
        lower = lax.slice_in_dim(padded, 4 - shift_k, 4 - shift_k + length, axis=axis)
        total = total + coeffs[shift_k] * (upper + lower)
    return total


def pad_axis(field, axis, width):
    widths = [(0, 0)] * field.ndim
    widths[axis] = (width, width)
    return jnp.pad(field, widths)


def merged_diff(field, depth):
    length = field.shape[-1]
    last = field.ndim - 1
    wide = pad_axis(field, last, 4 * depth)
    total = 2.0 * coeffs[0] * field
    for shift_k in range(1, 5):
        upper = lax.slice_in_dim(wide, 4 * depth + shift_k * depth, 4 * depth + shift_k * depth + length, axis=last)
        lower = lax.slice_in_dim(wide, 4 * depth - shift_k * depth, 4 * depth - shift_k * depth + length, axis=last)
        total = total + coeffs[shift_k] * (upper + lower)
    narrow = pad_axis(field, last, 4)
    position = jnp.arange(length, dtype=jnp.int32) % depth
    for shift_k in range(1, 5):
        upper = lax.slice_in_dim(narrow, 4 + shift_k, 4 + shift_k + length, axis=last)
        lower = lax.slice_in_dim(narrow, 4 - shift_k, 4 - shift_k + length, axis=last)
        upper_mask = (position + shift_k < depth).astype(field.dtype)
        lower_mask = (position - shift_k >= 0).astype(field.dtype)
        total = total + coeffs[shift_k] * (upper * upper_mask + lower * lower_mask)
    return total


def scaled(field, potential):
    lap = second_diff(pad_axis(field, 1, 4), 1, field.shape[1])
    lap = lap + merged_diff(field, NZ)
    return (kinetic * lap + (potential[None] - center) * field) / half_width


def filter_block(block, potential):
    previous = block
    current = scaled(block, potential)
    for step in range(3):
        previous, current = current, 2.0 * scaled(current, potential) - previous
    image = scaled(current, potential)
    return current, current.astype(jnp.bfloat16), image.astype(jnp.bfloat16)


def reference(orbitals, potential):
    group = math.gcd(ORB, 64)
    blocks = orbitals.reshape(ORB // group, group, NX, NY * NZ)
    filtered, low, image = lax.map(lambda blk: filter_block(blk, potential), blocks)
    filtered = filtered.reshape(ORB, NX, NY * NZ)
    low_flat = low.reshape(ORB, NCELLS).astype(jnp.float32)
    image_flat = image.reshape(ORB, NCELLS).astype(jnp.float32)
    proj_ham = jnp.dot(low_flat, image_flat.T, precision=lax.Precision.HIGHEST) / NCELLS
    proj_intersection = jnp.dot(low_flat, low_flat.T, precision=lax.Precision.HIGHEST) / NCELLS
    return filtered, proj_ham, proj_intersection
```

```python
import functools

import jax
import jax.numpy as jnp
from jax import lax
from jax.experimental import pallas as pl
from jax.experimental.pallas import tpu as pltpu
from jax.sharding import PartitionSpec as P

NZ = 144
GROUP = 64
TILE = 16
PAD = 8
CUT = 72
PART = 80
FIRST_B = NZ - PART
VMEM_LIMIT = 40 << 20

coeffs = (-205.0 / 72.0, 8.0 / 5.0, -1.0 / 5.0, 8.0 / 315.0, -1.0 / 560.0)
kinetic = -0.5 / 0.09
center = 68.0
half_width = 48.0
scaled_coeffs = [kinetic * c / half_width for c in coeffs]
carry = [coeffs[k] / coeffs[k + 1] for k in range(1, 4)]

IN_VMEM = pl.BlockSpec(memory_space=pltpu.VMEM)
IN_SMEM = pl.BlockSpec(memory_space=pltpu.SMEM)


def rounded_planes(planes):
    sent, error = [], None
    for i, plane in enumerate(planes):
        value = plane if error is None else plane + carry[i - 1] * error
        low = value.astype(jnp.bfloat16)
        error = value - low.astype(jnp.float32)
        sent.append(low)
    return sent


def pack_kernel(chunks, field, *refs):
    outs, errors = refs[: 3 * chunks], refs[3 * chunks :]
    step = pl.program_id(0)
    rows = field[0]
    if rows.shape[0] < 128:
        rows = jnp.concatenate([rows, rows], axis=0)
    flipped = rows.T
    half = flipped.shape[0] // 2
    left = lax.broadcasted_iota(jnp.int32, (NZ, 128), 1) < GROUP
    place = lax.rem(step, 4)
    factor = jnp.where(
        place == 0, 0.0, jnp.where(place == 1, carry[0], jnp.where(place == 2, carry[1], carry[2]))
    ).astype(jnp.float32)

    @pl.when(step == 0)
    def _():
        for error in errors:
            error[...] = jnp.zeros_like(error)

    for y in range(half // NZ):
        near = flipped[y * NZ : (y + 1) * NZ]
        far = flipped[half + y * NZ : half + (y + 1) * NZ]
        for c in range(chunks):
            packed, below, above = outs[3 * c : 3 * c + 3]
            if chunks == 1:
                value = jnp.where(left, near, far)
            elif c == 0:
                value = jnp.where(left, near, pltpu.roll(far, GROUP, 1))
            else:
                value = jnp.where(left, pltpu.roll(near, GROUP, 1), far)
            packed[0, y, 0:PAD, :] = jnp.zeros((PAD, 128), jnp.float32)
            packed[0, y, NZ + PAD : NZ + 2 * PAD, :] = jnp.zeros((PAD, 128), jnp.float32)
            packed[0, y, PAD : NZ + PAD, :] = value
            wide = value + factor * errors[c][y]
            low = wide.astype(jnp.bfloat16)
            errors[c][y] = wide - low.astype(jnp.float32)

            @pl.when(step < 4)
            def _():
                below[step, y] = low

            @pl.when(jnp.logical_and(step >= 4, step < 8))
            def _():
                above[7 - step, y] = low


def pack(field, chunks):
    nx, rows, cells = field.shape
    ny = cells // NZ // 2

    def plane(s):
        return jnp.where(s < 4, s, jnp.where(s < 8, nx + 3 - s, s - 4))

    shapes, specs = [], []
    for _ in range(chunks):
        shapes.append(jax.ShapeDtypeStruct((nx, ny, NZ + 2 * PAD, 128), jnp.float32))
        specs.append(pl.BlockSpec((1, ny, NZ + 2 * PAD, 128), lambda s: (plane(s), 0, 0, 0)))
        for _ in range(2):
            shapes.append(jax.ShapeDtypeStruct((4, ny, NZ, 128), jnp.bfloat16))
            specs.append(pl.BlockSpec((4, ny, NZ, 128), lambda s: (0, 0, 0, 0)))
    return pl.pallas_call(
        functools.partial(pack_kernel, chunks),
        grid=(nx,),
        in_specs=[pl.BlockSpec((1, rows, cells), lambda s: (plane(s), 0, 0))],
        out_specs=specs,
        out_shape=shapes,
        scratch_shapes=[pltpu.VMEM((ny, NZ, 128), jnp.float32)] * chunks,
        compiler_params=pltpu.CompilerParams(vmem_limit_bytes=VMEM_LIMIT),
        name="pack",
    )(field)


def unpack_kernel(rows, *refs):
    chunks, out = refs[:-1], refs[-1]
    ny = chunks[0].shape[1]
    left = lax.broadcasted_iota(jnp.int32, (NZ, 128), 1) < GROUP
    near, far = [], []
    for y in range(ny):
        parts = [chunk[0, y, PAD : NZ + PAD, :] for chunk in chunks]
        if len(parts) == 1:
            near.append(parts[0])
            far.append(pltpu.roll(parts[0], GROUP, 1))
        else:
            near.append(jnp.where(left, parts[0], pltpu.roll(parts[1], GROUP, 1)))
            far.append(jnp.where(left, pltpu.roll(parts[0], GROUP, 1), parts[1]))
    out[0] = jnp.concatenate(near + far, axis=0).T[:rows]


def unpack(chunks, rows):
    nx, ny, depth, _ = chunks[0].shape
    cells = 2 * ny * NZ
    return pl.pallas_call(
        functools.partial(unpack_kernel, rows),
        grid=(nx,),
        in_specs=[pl.BlockSpec((1, ny, depth, 128), lambda s: (s, 0, 0, 0))] * len(chunks),
        out_specs=pl.BlockSpec((1, rows, cells), lambda s: (s, 0, 0)),
        out_shape=jax.ShapeDtypeStruct((nx, rows, cells), jnp.float32),
        compiler_params=pltpu.CompilerParams(vmem_limit_bytes=VMEM_LIMIT),
        name="unpack",
    )(*chunks)


def apply_kernel(mode, *refs):
    refs = list(refs)
    lower = refs.pop(0) if mode == "image" else None
    cur = refs.pop(0)
    prev = refs.pop(0) if mode in ("middle", "last") else None
    below, above, pot = refs.pop(0), refs.pop(0), refs.pop(0)
    nx, ny = cur.shape[:2]
    left = lax.broadcasted_iota(jnp.int32, (TILE, 128), 1) < GROUP
    if mode == "image":
        part_a, part_b, part_w = refs
    else:
        new, out_below, out_above = refs[:3]
        zero = jnp.zeros((PAD, 128), jnp.float32)
        for x in range(nx):
            for y in range(ny):
                new[x, y, 0:PAD, :] = zero
                new[x, y, NZ + PAD : NZ + 2 * PAD, :] = zero

    def body(t, in_a, in_b):
        z = pl.multiple_of(t * TILE, TILE)
        in_cut = lax.broadcasted_iota(jnp.int32, (TILE, 128), 0) + FIRST_B >= CUT

        def plane(x, y):
            if x < 0:
                return below[4 + x, y, pl.ds(z, TILE), :].astype(jnp.float32)
            if x >= nx:
                return above[x - nx, y, pl.ds(z, TILE), :].astype(jnp.float32)
            return cur[x, y, pl.ds(z + PAD, TILE), :]

        results = []
        for x in range(nx):
            mine = [plane(x, y) for y in range(ny)]
            other = [pltpu.roll(a, GROUP, 1) for a in mine]
            after = [jnp.where(left, a, 0.0) for a in other]
            before = [jnp.where(left, 0.0, a) for a in other]
            row = []
            for y in range(ny):
                total = pot[x, y, pl.ds(z, TILE), :] * mine[y]
                both = in_a and in_b and mode == "image"
                strip = jnp.zeros_like(total) if both else None
                for k in range(1, 5):
                    pairs = plane(x - k, y) + plane(x + k, y)
                    if k == ny:
                        pairs = pairs + other[y]
                    else:
                        up = mine[y + k] if y + k < ny else after[y + k - ny]
                        down = mine[y - k] if y >= k else before[y - k + ny]
                        pairs = pairs + (up + down)
                    forth = cur[x, y, pl.ds(z + PAD + k, TILE), :]
                    back = cur[x, y, pl.ds(z + PAD - k, TILE), :]
                    if both:
                        depth = lax.broadcasted_iota(jnp.int32, (TILE, 128), 0) + FIRST_B
                        cut = jnp.where(in_cut, pairs, 0.0) + jnp.where(depth + k >= CUT, forth, 0.0)
                        cut = cut + jnp.where(depth - k >= CUT, back, 0.0)
                        strip = strip + scaled_coeffs[k] * cut
                        if k == 1:
                            strip = strip + jnp.where(in_cut, total, 0.0)
                    pairs = pairs + (forth + back)
                    total = total + scaled_coeffs[k] * pairs
                if mode == "image":
                    low = mine[y].astype(jnp.bfloat16)
                    image = total.astype(jnp.bfloat16)
                    if both:
                        none = jnp.zeros_like(low)
                        keep_b = in_cut.astype(jnp.float32).astype(jnp.bfloat16)
                        keep_a = 1.0 - keep_b
                        part_a[x, y, pl.ds(z, TILE), 0:128] = image * keep_a
                        part_a[x, y, pl.ds(z, TILE), 128:256] = low * keep_a
                        part_b[x, y, 0:TILE, 0:128] = image * keep_b
                        part_b[x, y, 0:TILE, 128:256] = low * keep_b
                        whole = jnp.where(in_cut, total, 0.0)
                        chosen = jnp.where(lower[0] > 0, strip, whole).astype(jnp.bfloat16)
                        part_w[x, y, 0:TILE, 0:128] = chosen
                        part_w[x, y, 0:TILE, 128:256] = low * keep_b
                    elif in_a:
                        part_a[x, y, pl.ds(z, TILE), 0:128] = image
                        part_a[x, y, pl.ds(z, TILE), 128:256] = low
                    else:
                        for part in (part_b, part_w):
                            part[x, y, pl.ds(z - FIRST_B, TILE), 0:128] = image
                            part[x, y, pl.ds(z - FIRST_B, TILE), 128:256] = low
                    continue
                if prev is not None:
                    total = (total + total) - prev[x, y, pl.ds(z + PAD, TILE), :]
                new[x, y, pl.ds(z + PAD, TILE), :] = total
                if mode == "last":
                    low = total.astype(jnp.bfloat16)
                    if in_a:
                        refs[3][x, y, pl.ds(z, TILE), :] = low
                    if in_b:
                        refs[4][x, y, pl.ds(z - FIRST_B, TILE), :] = low
                row.append(total)
            results.append(row)
        if mode == "image":
            return
        for y in range(ny):
            for i, low in enumerate(rounded_planes([results[i][y] for i in range(4)])):
                out_below[i, y, pl.ds(z, TILE), :] = low
            for i, low in enumerate(rounded_planes([results[nx - 1 - i][y] for i in range(4)])):
                out_above[3 - i, y, pl.ds(z, TILE), :] = low

    def loop(start, stop, in_a, in_b):
        def step(t, _):
            body(t, in_a, in_b)
            return 0

        lax.fori_loop(start, stop, step, 0)

    if mode in ("first", "middle"):
        loop(0, NZ // TILE, False, False)
    else:
        loop(0, FIRST_B // TILE, True, False)
        loop(FIRST_B // TILE, PART // TILE, True, True)
        loop(PART // TILE, NZ // TILE, False, True)


def apply_op(mode, cur, prev, below, above, pot, lower=None):
    nx, ny = cur.shape[:2]
    edge = jax.ShapeDtypeStruct((4, ny, NZ, 128), jnp.bfloat16)
    part = jax.ShapeDtypeStruct((nx, ny, PART, 128), jnp.bfloat16)
    wide = jax.ShapeDtypeStruct((nx, ny, PART, 256), jnp.bfloat16)
    shapes = [jax.ShapeDtypeStruct(cur.shape, cur.dtype), edge, edge]
    if mode == "last":
        shapes = shapes + [part, part]
    if mode == "image":
        shapes = [wide, wide, wide]
    args = [cur] + ([prev] if prev is not None else []) + [below, above, pot]
    specs = [IN_VMEM] * len(args)
    if mode == "image":
        args, specs = [lower] + args, [IN_SMEM] + specs
    return pl.pallas_call(
        functools.partial(apply_kernel, mode),
        in_specs=specs,
        out_specs=[IN_VMEM] * len(shapes),
        out_shape=shapes,
        compiler_params=pltpu.CompilerParams(vmem_limit_bytes=VMEM_LIMIT),
        cost_estimate=pl.CostEstimate(
            flops=30 * cur.size, bytes_accessed=4 * cur.size, transcendentals=0
        ),
        name="apply_" + mode,
    )(*args)


def exchange(below, above):
    count = lax.axis_size("domain")
    up = [(i, i + 1) for i in range(count - 1)]
    down = [(i + 1, i) for i in range(count - 1)]
    return lax.ppermute(above, "domain", up), lax.ppermute(below, "domain", down)


def product(left, right):
    full = lax.dot_general(
        left, right, (((0, 1, 2), (0, 1, 2)), ((), ())), preferred_element_type=jnp.float32
    ).reshape(2, GROUP, 2, 2, GROUP)
    return full[0, :, :, 0] + full[1, :, :, 1]


def gathered_products(lows, rights):
    bands = lax.axis_size("band")
    mid = bands // 2
    chunks = len(lows)

    def table(left, right):
        return jnp.concatenate([product(left, right[c]) for c in range(chunks)], axis=-1)

    slots = []
    for c in range(chunks):
        low_a, low_b = lows[c]
        sums = [None] * bands

        def add(slot, value):
            sums[slot] = value if sums[slot] is None else sums[slot] + value

        add(0, table(low_a, rights["a"]) + table(low_b, rights["b"]))
        right_a, right_b, left_a, left_b = low_a, low_b, low_a, low_b
        for hop in range(1, bands):
            pairs = [(b - 1, b) for b in range(hop, bands) if b - hop < mid]
            right_a = lax.ppermute(right_a, "band", pairs)
            add(bands - hop, table(right_a, rights["a"]))
            pairs = [(b + 1, b) for b in range(bands - hop) if b + hop >= mid]
            left_b = lax.ppermute(left_b, "band", pairs)
            add(hop, table(left_b, rights["w"]))
            pairs = [(b - 1, b) for b in range(hop, mid)]
            if pairs:
                right_b = lax.ppermute(right_b, "band", pairs)
                add(bands - hop, table(right_b, rights["b"]))
            pairs = [(b + 1, b) for b in range(mid, bands - hop)]
            if pairs:
                left_a = lax.ppermute(left_a, "band", pairs)
                add(hop, table(left_a, rights["a"]))
        slots.append(jnp.stack(sums))
    return jnp.concatenate(slots, axis=1)


def summed_over_domain(table):
    count = lax.axis_size("domain")
    me = lax.axis_index("domain")
    bit = 1
    table = table.reshape((count, table.shape[0] // count) + table.shape[1:])
    while bit < count:
        groups = table.reshape((table.shape[0] // 2, 2) + table.shape[1:])
        mine = lax.rem(me // bit, 2)
        keep = lax.dynamic_index_in_dim(groups, mine, axis=1, keepdims=False)
        send = lax.dynamic_index_in_dim(groups, 1 - mine, axis=1, keepdims=False)
        table = keep + lax.ppermute(send, "domain", [(i, i ^ bit) for i in range(count)])
        bit *= 2
    return table[0]


def other_triangle(table):
    bands, count = lax.axis_size("band"), lax.axis_size("domain")
    d, b = lax.axis_index("domain"), lax.axis_index("band")
    ratio = count // bands
    rows = table.shape[0]
    place = lax.rem(d, ratio)
    pieces = []
    for shift in range(ratio):
        to = lax.rem(place + shift, ratio)
        block = lax.dynamic_slice_in_dim(table, to * rows, rows, axis=2)
        pairs = []
        for i in range(count):
            for j in range(bands):
                target = ratio * j + (i % ratio + shift) % ratio
                pairs.append((i * bands + j, target * bands + i // ratio))
        pieces.append(lax.ppermute(block, ("domain", "band"), pairs).transpose(2, 1, 0))
    ordered = [
        lax.dynamic_index_in_dim(
            jnp.stack(pieces), lax.rem(place - t + ratio, ratio), axis=0, keepdims=False
        )
        for t in range(ratio)
    ]
    out = jnp.concatenate(ordered, axis=2)
    return jnp.where(d // ratio == b, 0.0, out)


def shards(orbitals, potential):
    own, nx, cells = orbitals.shape
    chunks = own // GROUP
    ny = cells // NZ // 2
    bands = lax.axis_size("band")
    total_cells = lax.axis_size("domain") * potential.size

    diagonal = (3.0 * kinetic * coeffs[0] + potential - center) / half_width
    diagonal = diagonal.reshape(nx, 2, ny, NZ).transpose(0, 2, 3, 1)
    pot = jnp.broadcast_to(diagonal[..., None], (nx, ny, NZ, 2, GROUP)).reshape(nx, ny, NZ, 128)

    packed = pack(orbitals.transpose(1, 0, 2), chunks)
    cur = [packed[3 * c] for c in range(chunks)]
    edges = [(packed[3 * c + 1], packed[3 * c + 2]) for c in range(chunks)]
    prev = [None] * chunks
    lows = [None] * chunks
    for step in range(4):
        mode = "first" if step == 0 else ("last" if step == 3 else "middle")
        for c in range(chunks):
            below, above = exchange(*edges[c])
            out = apply_op(mode, cur[c], prev[c], below, above, pot)
            prev[c], cur[c], edges[c] = cur[c], out[0], (out[1], out[2])
            lows[c] = out[3:]
    filtered = unpack(cur, own).transpose(1, 0, 2)

    lower = (lax.axis_index("band") < bands // 2).astype(jnp.int32).reshape(1)
    rights = {"a": [], "b": [], "w": []}
    for c in range(chunks):
        below, above = exchange(*edges[c])
        for name, part in zip("abw", apply_op("image", cur[c], None, below, above, pot, lower)):
            rights[name].append(part)

    table = gathered_products(lows, rights)
    table = jnp.roll(table, lax.axis_index("band"), axis=0)
    table = summed_over_domain(table.reshape((bands * own,) + table.shape[2:]))
    table = (table + other_triangle(table)) / total_cells
    return (filtered, table[:, 0], table[:, 1])


def solution(mesh):
    placed = (P("band", "domain", None), P("domain", None))
    return jax.shard_map(
        shards,
        mesh=mesh,
        in_specs=placed,
        out_specs=(P("band", "domain", None), P("domain", "band"), P("domain", "band")),
        check_vma=False,
    )
```

```python
import functools

import jax
import jax.numpy as jnp
from jax import lax
from jax.experimental import pallas as pl
from jax.experimental.pallas import tpu as pltpu
from jax.sharding import PartitionSpec as P

NZ = 144
GROUP = 64
TILE = 16
PAD = 8
CUT = 72
PART = 80
FIRST_B = NZ - PART
VMEM_LIMIT = 40 << 20

coeffs = (-205.0 / 72.0, 8.0 / 5.0, -1.0 / 5.0, 8.0 / 315.0, -1.0 / 560.0)
kinetic = -0.5 / 0.09
center = 68.0
half_width = 48.0
scaled_coeffs = [kinetic * c / half_width for c in coeffs]
carry = [coeffs[k] / coeffs[k + 1] for k in range(1, 4)]

IN_VMEM = pl.BlockSpec(memory_space=pltpu.VMEM)
ANYWHERE = pl.BlockSpec(memory_space=pl.ANY)
IN_SMEM = pl.BlockSpec(memory_space=pltpu.SMEM)


def rounded_planes(planes):
    sent, error = [], None
    for i, plane in enumerate(planes):
        value = plane if error is None else plane + carry[i - 1] * error
        low = value.astype(jnp.bfloat16)
        error = value - low.astype(jnp.float32)
        sent.append(low)
    return sent


def pack_kernel(chunks, field, *refs):
    outs, errors = refs[: 3 * chunks], refs[3 * chunks :]
    step = pl.program_id(0)
    rows = field[0]
    if rows.shape[0] < 128:
        rows = jnp.concatenate([rows, rows], axis=0)
    flipped = rows.T
    half = flipped.shape[0] // 2
    left = lax.broadcasted_iota(jnp.int32, (NZ, 128), 1) < GROUP
    place = lax.rem(step, 4)
    factor = jnp.where(
        place == 0, 0.0, jnp.where(place == 1, carry[0], jnp.where(place == 2, carry[1], carry[2]))
    ).astype(jnp.float32)

    @pl.when(step == 0)
    def _():
        for error in errors:
            error[...] = jnp.zeros_like(error)

    for y in range(half // NZ):
        near = flipped[y * NZ : (y + 1) * NZ]
        far = flipped[half + y * NZ : half + (y + 1) * NZ]
        for c in range(chunks):
            packed, below, above = outs[3 * c : 3 * c + 3]
            if chunks == 1:
                value = jnp.where(left, near, far)
            elif c == 0:
                value = jnp.where(left, near, pltpu.roll(far, GROUP, 1))
            else:
                value = jnp.where(left, pltpu.roll(near, GROUP, 1), far)
            packed[0, y, 0:PAD, :] = jnp.zeros((PAD, 128), jnp.float32)
            packed[0, y, NZ + PAD : NZ + 2 * PAD, :] = jnp.zeros((PAD, 128), jnp.float32)
            packed[0, y, PAD : NZ + PAD, :] = value
            wide = value + factor * errors[c][y]
            low = wide.astype(jnp.bfloat16)
            errors[c][y] = wide - low.astype(jnp.float32)

            @pl.when(step < 4)
            def _():
                below[step, y] = low

            @pl.when(jnp.logical_and(step >= 4, step < 8))
            def _():
                above[7 - step, y] = low


def pack(field, chunks):
    nx, rows, cells = field.shape
    ny = cells // NZ // 2

    def plane(s):
        return jnp.where(s < 4, s, jnp.where(s < 8, nx + 3 - s, s - 4))

    shapes, specs = [], []
    for _ in range(chunks):
        shapes.append(jax.ShapeDtypeStruct((nx, ny, NZ + 2 * PAD, 128), jnp.float32))
        specs.append(pl.BlockSpec((1, ny, NZ + 2 * PAD, 128), lambda s: (plane(s), 0, 0, 0)))
        for _ in range(2):
            shapes.append(jax.ShapeDtypeStruct((4, ny, NZ, 128), jnp.bfloat16))
            specs.append(pl.BlockSpec((4, ny, NZ, 128), lambda s: (0, 0, 0, 0)))
    return pl.pallas_call(
        functools.partial(pack_kernel, chunks),
        grid=(nx,),
        in_specs=[pl.BlockSpec((1, rows, cells), lambda s: (plane(s), 0, 0))],
        out_specs=specs,
        out_shape=shapes,
        scratch_shapes=[pltpu.VMEM((ny, NZ, 128), jnp.float32)] * chunks,
        compiler_params=pltpu.CompilerParams(vmem_limit_bytes=VMEM_LIMIT),
        name="pack",
    )(field)


def unpack_kernel(rows, count, *refs):
    chunks, out = refs[:count], refs[-1]
    ny = chunks[0].shape[1]
    left = lax.broadcasted_iota(jnp.int32, (NZ, 128), 1) < GROUP
    near, far = [], []
    for y in range(ny):
        parts = [chunk[0, y, PAD : NZ + PAD, :] for chunk in chunks]
        if len(parts) == 1:
            near.append(parts[0])
            far.append(pltpu.roll(parts[0], GROUP, 1))
        else:
            near.append(jnp.where(left, parts[0], pltpu.roll(parts[1], GROUP, 1)))
            far.append(jnp.where(left, pltpu.roll(parts[0], GROUP, 1), parts[1]))
    out[0] = jnp.concatenate(near + far, axis=0).T[:rows]


def unpack(chunks, rows, after=()):
    nx, ny, depth, _ = chunks[0].shape
    cells = 2 * ny * NZ
    return pl.pallas_call(
        functools.partial(unpack_kernel, rows, len(chunks)),
        grid=(nx,),
        in_specs=[pl.BlockSpec((1, ny, depth, 128), lambda s: (s, 0, 0, 0))] * len(chunks)
        + [ANYWHERE] * len(after),
        out_specs=pl.BlockSpec((1, rows, cells), lambda s: (s, 0, 0)),
        out_shape=jax.ShapeDtypeStruct((nx, rows, cells), jnp.float32),
        compiler_params=pltpu.CompilerParams(vmem_limit_bytes=VMEM_LIMIT),
        name="unpack",
    )(*chunks, *after)


def apply_kernel(mode, *refs):
    refs = list(refs)
    lower = refs.pop(0) if mode == "image" else None
    cur = refs.pop(0)
    prev = refs.pop(0) if mode in ("middle", "last") else None
    below, above, pot = refs.pop(0), refs.pop(0), refs.pop(0)
    nx, ny = cur.shape[:2]
    left = lax.broadcasted_iota(jnp.int32, (TILE, 128), 1) < GROUP
    if mode == "image":
        part_a, part_b, part_w = refs
    else:
        new, out_below, out_above = refs[:3]
        zero = jnp.zeros((PAD, 128), jnp.float32)
        for x in range(nx):
            for y in range(ny):
                new[x, y, 0:PAD, :] = zero
                new[x, y, NZ + PAD : NZ + 2 * PAD, :] = zero

    def body(t, in_a, in_b):
        z = pl.multiple_of(t * TILE, TILE)
        in_cut = lax.broadcasted_iota(jnp.int32, (TILE, 128), 0) + FIRST_B >= CUT

        def plane(x, y):
            if x < 0:
                return below[4 + x, y, pl.ds(z, TILE), :].astype(jnp.float32)
            if x >= nx:
                return above[x - nx, y, pl.ds(z, TILE), :].astype(jnp.float32)
            return cur[x, y, pl.ds(z + PAD, TILE), :]

        results = []
        for x in range(nx):
            mine = [plane(x, y) for y in range(ny)]
            other = [pltpu.roll(a, GROUP, 1) for a in mine]
            after = [jnp.where(left, a, 0.0) for a in other]
            before = [jnp.where(left, 0.0, a) for a in other]
            row = []
            for y in range(ny):
                total = pot[x, y, pl.ds(z, TILE), :] * mine[y]
                both = in_a and in_b and mode == "image"
                strip = jnp.zeros_like(total) if both else None
                for k in range(1, 5):
                    pairs = plane(x - k, y) + plane(x + k, y)
                    if k == ny:
                        pairs = pairs + other[y]
                    else:
                        up = mine[y + k] if y + k < ny else after[y + k - ny]
                        down = mine[y - k] if y >= k else before[y - k + ny]
                        pairs = pairs + (up + down)
                    forth = cur[x, y, pl.ds(z + PAD + k, TILE), :]
                    back = cur[x, y, pl.ds(z + PAD - k, TILE), :]
                    if both:
                        depth = lax.broadcasted_iota(jnp.int32, (TILE, 128), 0) + FIRST_B
                        cut = jnp.where(in_cut, pairs, 0.0) + jnp.where(depth + k >= CUT, forth, 0.0)
                        cut = cut + jnp.where(depth - k >= CUT, back, 0.0)
                        strip = strip + scaled_coeffs[k] * cut
                        if k == 1:
                            strip = strip + jnp.where(in_cut, total, 0.0)
                    pairs = pairs + (forth + back)
                    total = total + scaled_coeffs[k] * pairs
                if mode == "image":
                    low = mine[y].astype(jnp.bfloat16)
                    image = total.astype(jnp.bfloat16)
                    if both:
                        none = jnp.zeros_like(low)
                        keep_b = in_cut.astype(jnp.float32).astype(jnp.bfloat16)
                        keep_a = 1.0 - keep_b
                        part_a[x, y, pl.ds(z, TILE), 0:128] = image * keep_a
                        part_a[x, y, pl.ds(z, TILE), 128:256] = low * keep_a
                        part_b[x, y, 0:TILE, 0:128] = image * keep_b
                        part_b[x, y, 0:TILE, 128:256] = low * keep_b
                        whole = jnp.where(in_cut, total, 0.0)
                        chosen = jnp.where(lower[0] > 0, strip, whole).astype(jnp.bfloat16)
                        part_w[x, y, 0:TILE, 0:128] = chosen
                        part_w[x, y, 0:TILE, 128:256] = low * keep_b
                    elif in_a:
                        part_a[x, y, pl.ds(z, TILE), 0:128] = image
                        part_a[x, y, pl.ds(z, TILE), 128:256] = low
                    else:
                        for part in (part_b, part_w):
                            part[x, y, pl.ds(z - FIRST_B, TILE), 0:128] = image
                            part[x, y, pl.ds(z - FIRST_B, TILE), 128:256] = low
                    continue
                if prev is not None:
                    total = (total + total) - prev[x, y, pl.ds(z + PAD, TILE), :]
                new[x, y, pl.ds(z + PAD, TILE), :] = total
                if mode == "last":
                    low = total.astype(jnp.bfloat16)
                    if in_a:
                        refs[3][x, y, pl.ds(z, TILE), :] = low
                    if in_b:
                        refs[4][x, y, pl.ds(z - FIRST_B, TILE), :] = low
                row.append(total)
            results.append(row)
        if mode == "image":
            return
        for y in range(ny):
            for i, low in enumerate(rounded_planes([results[i][y] for i in range(4)])):
                out_below[i, y, pl.ds(z, TILE), :] = low
            for i, low in enumerate(rounded_planes([results[nx - 1 - i][y] for i in range(4)])):
                out_above[3 - i, y, pl.ds(z, TILE), :] = low

    def loop(start, stop, in_a, in_b):
        def step(t, _):
            body(t, in_a, in_b)
            return 0

        lax.fori_loop(start, stop, step, 0)

    if mode in ("first", "middle"):
        loop(0, NZ // TILE, False, False)
    else:
        loop(0, FIRST_B // TILE, True, False)
        loop(FIRST_B // TILE, PART // TILE, True, True)
        loop(PART // TILE, NZ // TILE, False, True)


def apply_op(mode, cur, prev, below, above, pot, lower=None):
    nx, ny = cur.shape[:2]
    edge = jax.ShapeDtypeStruct((4, ny, NZ, 128), jnp.bfloat16)
    part = jax.ShapeDtypeStruct((nx, ny, PART, 128), jnp.bfloat16)
    wide = jax.ShapeDtypeStruct((nx, ny, PART, 256), jnp.bfloat16)
    shapes = [jax.ShapeDtypeStruct(cur.shape, cur.dtype), edge, edge]
    if mode == "last":
        shapes = shapes + [part, part]
    if mode == "image":
        shapes = [wide, wide, wide]
    args = [cur] + ([prev] if prev is not None else []) + [below, above, pot]
    specs = [IN_VMEM] * len(args)
    if mode == "image":
        args, specs = [lower] + args, [IN_SMEM] + specs
    return pl.pallas_call(
        functools.partial(apply_kernel, mode),
        in_specs=specs,
        out_specs=[IN_VMEM] * len(shapes),
        out_shape=shapes,
        compiler_params=pltpu.CompilerParams(vmem_limit_bytes=VMEM_LIMIT),
        cost_estimate=pl.CostEstimate(
            flops=30 * cur.size, bytes_accessed=4 * cur.size, transcendentals=0
        ),
        name="apply_" + mode,
    )(*args)


def exchange(below, above):
    count = lax.axis_size("domain")
    up = [(i, i + 1) for i in range(count - 1)]
    down = [(i + 1, i) for i in range(count - 1)]
    return lax.ppermute(above, "domain", up), lax.ppermute(below, "domain", down)


def gram_kernel(kinds, chunks, has_sums, *refs):
    plan, refs = refs[0], refs[1:]
    blocks, refs = refs[: len(kinds)], refs[len(kinds) :]
    rights, refs = refs[: 3 * chunks], refs[3 * chunks :]
    sums = refs[0] if has_sums else None
    out, full = refs[-2], refs[-1]
    left = lax.broadcasted_iota(jnp.int32, (GROUP, 128), 1) < GROUP
    out[...] = sums[...] if has_sums else jnp.zeros_like(out)
    depth = blocks[0].shape[0]
    part = depth // 3

    def one(block, kind, slot):
        full[...] = jnp.zeros_like(full)

        def step(i, _):
            rows = pl.ds(pl.multiple_of(i * part, 16), part)
            for c in range(chunks):
                full[c] += lax.dot_general(
                    block[rows, :],
                    rights[3 * c + kind][rows, :],
                    (((0,), (0,)), ((), ())),
                    preferred_element_type=jnp.float32,
                )
            return 0

        lax.fori_loop(0, 3, step, 0)
        for m in range(2):
            lanes = slice(128 * m, 128 * (m + 1))
            value = full[0, 0:GROUP, lanes] + pltpu.roll(full[0, GROUP:128, lanes], GROUP, 1)
            if chunks == 2:
                second = pltpu.roll(full[1, 0:GROUP, lanes], GROUP, 1) + full[1, GROUP:128, lanes]
                value = jnp.where(left, value, second)
            out[m, slot] += value

    for i, choices in enumerate(kinds):
        for kind in choices:

            @pl.when(plan[2 * i] == kind)
            def _():
                one(blocks[i], kind, plan[2 * i + 1])


def gram(blocks, kinds, plan, rights, sums, bands, after=()):
    chunks = len(rights)
    flat = [block.reshape(-1, 128) for block in blocks]
    flat = flat + [part.reshape(-1, 256) for three in rights for part in three]
    if sums is not None:
        flat.append(sums)
    shape = (2, bands, GROUP, 128)
    kernel = functools.partial(gram_kernel, kinds, chunks, sums is not None)
    return pl.pallas_call(
        lambda plan, *refs: kernel(plan, *refs[: len(flat)], *refs[len(flat) + len(after) :]),
        in_specs=[IN_SMEM] + [IN_VMEM] * len(flat) + [ANYWHERE] * len(after),
        out_specs=IN_VMEM,
        out_shape=jax.ShapeDtypeStruct(shape, jnp.float32),
        scratch_shapes=[pltpu.VMEM((chunks, 128, 256), jnp.float32)],
        compiler_params=pltpu.CompilerParams(vmem_limit_bytes=VMEM_LIMIT),
        name="gram",
    )(plan, *flat, *after)


def hops(low_a, low_b):
    bands = lax.axis_size("band")
    band = lax.axis_index("band")
    mid = bands // 2
    up, down = low_a, low_b
    ups, downs = [], []
    for hop in range(1, bands):
        pairs = [b for b in range(hop, bands) if b - hop < mid]
        if hop >= mid:
            pairs = pairs + list(range(hop - mid + 1, mid))
        if hop == mid and mid > 1:
            up = jnp.where(band < mid - 1, low_b, up)
            down = jnp.where(band > bands - mid, low_a, down)
        up = lax.ppermute(up, "band", [(b - 1, b) for b in pairs])
        down = lax.ppermute(down, "band", [(bands - b, bands - 1 - b) for b in pairs])
        ups.append(up)
        downs.append(down)
    return ups, downs


def hop_plan(hop, bands, band):
    mid = bands // 2
    late = hop - mid + 1
    skip = 3

    def one(place, main, other, sign):
        is_main = jnp.logical_and(place >= hop, place - hop < mid)
        is_late = jnp.logical_and(hop >= mid, jnp.logical_and(place >= late, place < mid))
        kind = jnp.where(is_main, main, jnp.where(is_late, other, skip))
        slot = band - sign * jnp.where(is_main, hop, jnp.where(is_late, late, 0))
        return [kind, slot]

    return one(band, 0, 1, 1) + one(bands - 1 - band, 2, 0, -1)


def summed_over_domain(table):
    count = lax.axis_size("domain")
    me = lax.axis_index("domain")
    bit = 1
    table = table.reshape(2, count, table.shape[1] // count, table.shape[2])
    while bit < count:
        groups = table.reshape((2, table.shape[1] // 2, 2) + table.shape[2:])
        mine = lax.rem(me // bit, 2)
        keep = lax.dynamic_index_in_dim(groups, mine, axis=2, keepdims=False)
        send = lax.dynamic_index_in_dim(groups, 1 - mine, axis=2, keepdims=False)
        table = keep + lax.ppermute(send, "domain", [(i, i ^ bit) for i in range(count)])
        bit *= 2
    return table[:, 0]


def other_triangle(table):
    bands, count = lax.axis_size("band"), lax.axis_size("domain")
    d, b = lax.axis_index("domain"), lax.axis_index("band")
    ratio = count // bands
    rows = table.shape[1]
    place = lax.rem(d, ratio)
    pieces = []
    for shift in range(ratio):
        to = lax.rem(place + shift, ratio)
        block = lax.dynamic_slice_in_dim(table, to * rows, rows, axis=2)
        pairs = []
        for i in range(count):
            for j in range(bands):
                target = ratio * j + (i % ratio + shift) % ratio
                pairs.append((i * bands + j, target * bands + i // ratio))
        pieces.append(lax.ppermute(block, ("domain", "band"), pairs).transpose(0, 2, 1))
    ordered = [
        lax.dynamic_index_in_dim(
            jnp.stack(pieces), lax.rem(place - t + ratio, ratio), axis=0, keepdims=False
        )
        for t in range(ratio)
    ]
    out = jnp.concatenate(ordered, axis=2)
    return jnp.where(d // ratio == b, 0.0, out)


def pot_kernel(diagonal, out):
    row = diagonal[0]
    half = row.shape[1] // 2
    wide = -(-half // 128) * 128
    first = lax.broadcasted_iota(jnp.int32, (128, wide), 0) < GROUP
    near = jnp.broadcast_to(row[:, :wide], (128, wide))
    far = jnp.broadcast_to(pltpu.roll(row, half, 1)[:, :wide], (128, wide))
    flipped = jnp.where(first, near, far).T
    for y in range(out.shape[1]):
        out[0, y] = flipped[y * NZ : (y + 1) * NZ]


def spread(diagonal):
    nx, cells = diagonal.shape
    ny = cells // NZ // 2
    return pl.pallas_call(
        pot_kernel,
        grid=(nx,),
        in_specs=[pl.BlockSpec((1, 1, cells), lambda s: (s, 0, 0))],
        out_specs=pl.BlockSpec((1, ny, NZ, 128), lambda s: (s, 0, 0, 0)),
        out_shape=jax.ShapeDtypeStruct((nx, ny, NZ, 128), jnp.float32),
        name="spread",
    )(diagonal.reshape(nx, 1, cells))


def shards(orbitals, potential):
    own, nx, cells = orbitals.shape
    chunks = own // GROUP
    bands = lax.axis_size("band")
    total_cells = lax.axis_size("domain") * potential.size

    pot = spread((3.0 * kinetic * coeffs[0] + potential - center) / half_width)

    packed = pack(orbitals.transpose(1, 0, 2), chunks)
    cur = [packed[3 * c] for c in range(chunks)]
    edges = [(packed[3 * c + 1], packed[3 * c + 2]) for c in range(chunks)]
    prev = [None] * chunks
    lows = [None] * chunks
    for step in range(4):
        mode = "first" if step == 0 else ("last" if step == 3 else "middle")
        for c in range(chunks):
            below, above = exchange(*edges[c])
            out = apply_op(mode, cur[c], prev[c], below, above, pot)
            prev[c], cur[c], edges[c] = cur[c], out[0], (out[1], out[2])
            lows[c] = out[3:]
    band = lax.axis_index("band")
    lower = (band < bands // 2).astype(jnp.int32).reshape(1)
    moved = [hops(*lows[c]) for c in range(chunks)]
    rights = []
    for c in range(chunks):
        below, above = exchange(*edges[c])
        rights.append(apply_op("image", cur[c], None, below, above, pot, lower))
    filtered = unpack(cur, own, after=[rights[-1][0]])

    own_plan = [jnp.int32(0), band, jnp.int32(1), band]
    plans = [hop_plan(hop, bands, band) for hop in range(1, bands)]
    kinds = [((0,), (2,)) if hop < bands // 2 else ((0, 1), (2, 0)) for hop in range(1, bands)]
    tables = []
    for c in range(chunks):
        ups, downs = moved[c]
        blocks = list(lows[c])
        plan, choice = list(own_plan), [(0,), (1,)]
        sums = None
        for i in range(bands - 1):
            blocks += [ups[i], downs[i]]
            plan += plans[i]
            choice += kinds[i]
            if i == bands - 2 or (c == chunks - 1 and i == bands - 3):
                rows = jnp.stack(plan).astype(jnp.int32)
                sums = gram(blocks, tuple(choice), rows, rights, sums, bands)
                blocks, plan, choice = [], [], []
        tables.append(sums)
    table = jnp.stack(tables, axis=2).reshape(2, bands * own, 128)[:, :, :own]
    table = summed_over_domain(table)
    table = (table + other_triangle(table)) / total_cells
    return (filtered.transpose(1, 0, 2), table[0], table[1])


def solution(mesh):
    placed = (P("band", "domain", None), P("domain", None))
    return jax.shard_map(
        shards,
        mesh=mesh,
        in_specs=placed,
        out_specs=(P("band", "domain", None), P("domain", "band"), P("domain", "band")),
        check_vma=False,
    )
```

```python
import functools

import jax
import jax.numpy as jnp
from jax import lax
from jax.experimental import pallas as pl
from jax.experimental.pallas import tpu as pltpu
from jax.sharding import PartitionSpec as P

NZ = 144
GROUP = 64
TILE = 16
PAD = 8
CUT = 72
PART = 80
FIRST_B = NZ - PART
SMALL_LIMIT = 6 << 20
GRAM_LIMIT = 10 << 20

coeffs = (-205.0 / 72.0, 8.0 / 5.0, -1.0 / 5.0, 8.0 / 315.0, -1.0 / 560.0)
kinetic = -0.5 / 0.09
center = 68.0
half_width = 48.0
scaled_coeffs = [kinetic * c / half_width for c in coeffs]
carry = [coeffs[k] / coeffs[k + 1] for k in range(1, 4)]

limits = {"first": 12 << 20, "middle": 15 << 20, "last": 19 << 20, "image": 14 << 20}

IN_VMEM = pl.BlockSpec(memory_space=pltpu.VMEM)
ANYWHERE = pl.BlockSpec(memory_space=pl.ANY)
IN_SMEM = pl.BlockSpec(memory_space=pltpu.SMEM)


def cost(moved):
    return pl.CostEstimate(flops=0, bytes_accessed=moved, transcendentals=0)


def rounded_planes(planes):
    sent, error = [], None
    for i, plane in enumerate(planes):
        value = plane if error is None else plane + carry[i - 1] * error
        low = value.astype(jnp.bfloat16)
        error = value - low.astype(jnp.float32)
        sent.append(low)
    return sent


def halves(rows):
    half = rows.shape[1] // 2
    wide = -(-half // 128) * 128
    far = pltpu.roll(rows, half, 1)
    return jnp.concatenate([rows[:, :wide], far[:, :wide]], axis=0).T


def pack_kernel(field, packed, below, above, error):
    step = pl.program_id(0)
    flipped = halves(field[0])
    place = lax.rem(step, 4)
    factor = jnp.where(
        place == 0, 0.0, jnp.where(place == 1, carry[0], jnp.where(place == 2, carry[1], carry[2]))
    ).astype(jnp.float32)

    @pl.when(step == 0)
    def _():
        error[...] = jnp.zeros_like(error)

    for y in range(packed.shape[1]):
        value = flipped[y * NZ : (y + 1) * NZ]
        packed[0, y, 0:PAD, :] = jnp.zeros((PAD, 128), jnp.float32)
        packed[0, y, NZ + PAD : NZ + 2 * PAD, :] = jnp.zeros((PAD, 128), jnp.float32)
        packed[0, y, PAD : NZ + PAD, :] = value

        @pl.when(step < 8)
        def _():
            wide = value + factor * error[y]
            low = wide.astype(jnp.bfloat16)
            error[y] = wide - low.astype(jnp.float32)

            @pl.when(step < 4)
            def _():
                below[step, y] = low

            @pl.when(step >= 4)
            def _():
                above[7 - step, y] = low


def pack(field, chunk):
    nx, _, cells = field.shape
    ny = cells // NZ // 2

    def plane(s):
        return jnp.where(s < 4, s, jnp.where(s < 8, nx + 3 - s, s - 4))

    edge = jax.ShapeDtypeStruct((4, ny, NZ, 128), jnp.bfloat16)
    edge_spec = pl.BlockSpec((4, ny, NZ, 128), lambda s: (0, 0, 0, 0))
    return pl.pallas_call(
        pack_kernel,
        grid=(nx,),
        in_specs=[pl.BlockSpec((1, GROUP, cells), lambda s: (plane(s), chunk, 0))],
        out_specs=[
            pl.BlockSpec((1, ny, NZ + 2 * PAD, 128), lambda s: (plane(s), 0, 0, 0)),
            edge_spec,
            edge_spec,
        ],
        out_shape=[jax.ShapeDtypeStruct((nx, ny, NZ + 2 * PAD, 128), jnp.float32), edge, edge],
        scratch_shapes=[pltpu.VMEM((ny, NZ, 128), jnp.float32)],
        compiler_params=pltpu.CompilerParams(vmem_limit_bytes=SMALL_LIMIT),
        cost_estimate=cost(2 * GROUP * nx * cells * 8),
        name="pack",
    )(field)


def unpack_kernel(rows, count, *refs):
    chunks, out = refs[:count], refs[-1]
    ny = chunks[0].shape[1]
    left = lax.broadcasted_iota(jnp.int32, (NZ, 128), 1) < GROUP
    near, far = [], []
    for y in range(ny):
        parts = [chunk[0, y, PAD : NZ + PAD, :] for chunk in chunks]
        if len(parts) == 1:
            near.append(parts[0])
            far.append(pltpu.roll(parts[0], GROUP, 1))
        else:
            near.append(jnp.where(left, parts[0], pltpu.roll(parts[1], GROUP, 1)))
            far.append(jnp.where(left, pltpu.roll(parts[0], GROUP, 1), parts[1]))
    out[0] = jnp.concatenate(near + far, axis=0).T[:rows]


def unpack(chunks, rows, after=()):
    nx, ny, depth, _ = chunks[0].shape
    cells = 2 * ny * NZ
    return pl.pallas_call(
        functools.partial(unpack_kernel, rows, len(chunks)),
        grid=(nx,),
        in_specs=[pl.BlockSpec((1, ny, depth, 128), lambda s: (s, 0, 0, 0))] * len(chunks)
        + [ANYWHERE] * len(after),
        out_specs=pl.BlockSpec((1, rows, cells), lambda s: (s, 0, 0)),
        out_shape=jax.ShapeDtypeStruct((nx, rows, cells), jnp.float32),
        compiler_params=pltpu.CompilerParams(vmem_limit_bytes=SMALL_LIMIT),
        cost_estimate=cost(rows * nx * cells * 16),
        name="unpack",
    )(*chunks, *after)


def apply_kernel(mode, waits, earlier, chunk, *refs):
    refs = list(refs)
    copies = []
    if earlier:
        sems = refs.pop()
    lower = refs.pop(0) if mode == "image" else None
    cur = refs.pop(0)
    prev = refs.pop(0) if mode in ("middle", "last") else None
    below, above, pot = refs.pop(0), refs.pop(0), refs.pop(0)
    if chunk is not None:
        below, above = below.at[chunk], above.at[chunk]
    refs = refs[waits:]
    if earlier:
        copies = [pltpu.make_async_copy(refs[i], refs[3 + i].at[0], sems.at[i]) for i in range(2)]
        refs = refs[2:]
        refs[1:3] = [refs[1].at[1], refs[2].at[1]]
    for copy in copies:
        copy.start()
    nx, ny = cur.shape[:2]
    left = lax.broadcasted_iota(jnp.int32, (TILE, 128), 1) < GROUP
    if mode == "image":
        part_a, part_b, part_w = refs
    else:
        new, out_below, out_above = refs[:3]
        zero = jnp.zeros((PAD, 128), jnp.float32)
        for x in range(nx):
            for y in range(ny):
                new[x, y, 0:PAD, :] = zero
                new[x, y, NZ + PAD : NZ + 2 * PAD, :] = zero

    def body(t, in_a, in_b):
        z = pl.multiple_of(t * TILE, TILE)
        in_cut = lax.broadcasted_iota(jnp.int32, (TILE, 128), 0) + FIRST_B >= CUT

        def plane(x, y):
            if x < 0:
                return below[4 + x, y, pl.ds(z, TILE), :].astype(jnp.float32)
            if x >= nx:
                return above[x - nx, y, pl.ds(z, TILE), :].astype(jnp.float32)
            return cur[x, y, pl.ds(z + PAD, TILE), :]

        results = []
        for x in range(nx):
            mine = [plane(x, y) for y in range(ny)]
            other = [pltpu.roll(a, GROUP, 1) for a in mine]
            after = [jnp.where(left, a, 0.0) for a in other]
            before = [jnp.where(left, 0.0, a) for a in other]
            row = []
            for y in range(ny):
                total = pot[x, y, pl.ds(z, TILE), :] * mine[y]
                both = in_a and in_b and mode == "image"
                strip = jnp.zeros_like(total) if both else None
                for k in range(1, 5):
                    pairs = plane(x - k, y) + plane(x + k, y)
                    if k == ny:
                        pairs = pairs + other[y]
                    else:
                        up = mine[y + k] if y + k < ny else after[y + k - ny]
                        down = mine[y - k] if y >= k else before[y - k + ny]
                        pairs = pairs + (up + down)
                    forth = cur[x, y, pl.ds(z + PAD + k, TILE), :]
                    back = cur[x, y, pl.ds(z + PAD - k, TILE), :]
                    if both:
                        depth = lax.broadcasted_iota(jnp.int32, (TILE, 128), 0) + FIRST_B
                        cut = jnp.where(in_cut, pairs, 0.0) + jnp.where(depth + k >= CUT, forth, 0.0)
                        cut = cut + jnp.where(depth - k >= CUT, back, 0.0)
                        strip = strip + scaled_coeffs[k] * cut
                        if k == 1:
                            strip = strip + jnp.where(in_cut, total, 0.0)
                    pairs = pairs + (forth + back)
                    total = total + scaled_coeffs[k] * pairs
                if mode == "image":
                    low = mine[y].astype(jnp.bfloat16)
                    image = total.astype(jnp.bfloat16)
                    if both:
                        none = jnp.zeros_like(low)
                        keep_b = in_cut.astype(jnp.float32).astype(jnp.bfloat16)
                        keep_a = 1.0 - keep_b
                        part_a[x, y, pl.ds(z, TILE), 0:128] = image * keep_a
                        part_a[x, y, pl.ds(z, TILE), 128:256] = low * keep_a
                        part_b[x, y, 0:TILE, 0:128] = image * keep_b
                        part_b[x, y, 0:TILE, 128:256] = low * keep_b
                        whole = jnp.where(in_cut, total, 0.0)
                        chosen = jnp.where(lower[0] > 0, strip, whole).astype(jnp.bfloat16)
                        part_w[x, y, 0:TILE, 0:128] = chosen
                        part_w[x, y, 0:TILE, 128:256] = low * keep_b
                    elif in_a:
                        part_a[x, y, pl.ds(z, TILE), 0:128] = image
                        part_a[x, y, pl.ds(z, TILE), 128:256] = low
                    else:
                        for part in (part_b, part_w):
                            part[x, y, pl.ds(z - FIRST_B, TILE), 0:128] = image
                            part[x, y, pl.ds(z - FIRST_B, TILE), 128:256] = low
                    continue
                if prev is not None:
                    total = (total + total) - prev[x, y, pl.ds(z + PAD, TILE), :]
                new[x, y, pl.ds(z + PAD, TILE), :] = total
                if mode == "last":
                    low = total.astype(jnp.bfloat16)
                    if in_a:
                        refs[3][x, y, pl.ds(z, TILE), :] = low
                    if in_b:
                        refs[4][x, y, pl.ds(z - FIRST_B, TILE), :] = low
                row.append(total)
            results.append(row)
        if mode == "image":
            return
        for y in range(ny):
            for i, low in enumerate(rounded_planes([results[i][y] for i in range(4)])):
                out_below[i, y, pl.ds(z, TILE), :] = low
            for i, low in enumerate(rounded_planes([results[nx - 1 - i][y] for i in range(4)])):
                out_above[3 - i, y, pl.ds(z, TILE), :] = low

    def loop(start, stop, in_a, in_b):
        def step(t, _):
            body(t, in_a, in_b)
            return 0

        lax.fori_loop(start, stop, step, 0)

    if mode in ("first", "middle"):
        loop(0, NZ // TILE, False, False)
    else:
        loop(0, FIRST_B // TILE, True, False)
        loop(FIRST_B // TILE, PART // TILE, True, True)
        loop(PART // TILE, NZ // TILE, False, True)
    for copy in copies:
        copy.wait()


def apply_op(mode, cur, prev, below, above, pot, lower=None, after=(), earlier=(), chunk=None):
    nx, ny = cur.shape[:2]
    edge = jax.ShapeDtypeStruct(((2,) if earlier else ()) + (4, ny, NZ, 128), jnp.bfloat16)
    part = jax.ShapeDtypeStruct((nx, ny, PART, 128), jnp.bfloat16)
    wide = jax.ShapeDtypeStruct((nx, ny, PART, 256), jnp.bfloat16)
    shapes = [jax.ShapeDtypeStruct(cur.shape, cur.dtype), edge, edge]
    if mode == "last":
        shapes = shapes + [part, part]
    if mode == "image":
        shapes = [wide, wide, wide]
    args = [cur] + ([prev] if prev is not None else []) + [below, above, pot]
    specs = [IN_VMEM] * len(args)
    if mode == "image":
        args, specs = [lower] + args, [IN_SMEM] + specs
    args = args + list(after) + list(earlier)
    specs = specs + [ANYWHERE] * (len(after) + len(earlier))
    return pl.pallas_call(
        functools.partial(apply_kernel, mode, len(after), bool(earlier), chunk),
        in_specs=specs,
        out_specs=[IN_VMEM] * len(shapes),
        out_shape=shapes,
        scratch_shapes=[pltpu.SemaphoreType.DMA((2,))] if earlier else [],
        compiler_params=pltpu.CompilerParams(vmem_limit_bytes=limits[mode]),
        cost_estimate=cost(22 * cur.size),
        name="apply_" + mode,
    )(*args)


def exchange(below, above):
    count = lax.axis_size("domain")
    up = [(i, i + 1) for i in range(count - 1)]
    down = [(i + 1, i) for i in range(count - 1)]
    return lax.ppermute(above, "domain", up), lax.ppermute(below, "domain", down)


def gram_kernel(kinds, used, chunks, plan, *refs):
    count = len(kinds)
    blocks, refs = refs[: count * chunks], refs[count * chunks :]
    rights, refs = refs[: len(used) * chunks], refs[len(used) * chunks :]
    sums, out, full = refs[0], refs[-2], refs[-1]
    left = lax.broadcasted_iota(jnp.int32, (GROUP, 128), 1) < GROUP
    step = pl.program_id(0)

    for i, choices in enumerate(kinds):
        for kind in choices:

            @pl.when(plan[2 * i] == kind)
            def _():
                mine = blocks[chunks * i : chunks * (i + 1)]
                turned = jnp.concatenate([block[...].T for block in mine], axis=0)
                ours = [rights[len(used) * c + used.index(kind)][...] for c in range(chunks)]
                value = jnp.dot(
                    turned, jnp.concatenate(ours, axis=1), preferred_element_type=jnp.float32
                )

                @pl.when(step == 0)
                def _():
                    full[i] = value

                @pl.when(step > 0)
                def _():
                    full[i] += value

    @pl.when(step == pl.num_programs(0) - 1)
    def _():
        out[...] = sums[...]
        for i in range(count):

            @pl.when(plan[2 * i] < 3)
            def _():
                for other in range(chunks):
                    top = slice(128 * other, 128 * other + GROUP)
                    low = slice(128 * other + GROUP, 128 * (other + 1))
                    for m in range(2):
                        lanes = slice(128 * m, 128 * (m + 1))
                        value = full[i, top, lanes] + pltpu.roll(full[i, low, lanes], GROUP, 1)
                        if chunks == 2:
                            lanes = slice(256 + 128 * m, 256 + 128 * (m + 1))
                            second = pltpu.roll(full[i, top, lanes], GROUP, 1)
                            value = jnp.where(left, value, second + full[i, low, lanes])
                        out[m, plan[2 * i + 1], other] += value


def gram(blocks, kinds, plan, rights, sums, after=()):
    chunks = len(rights)
    steps = 6
    flat = [block.reshape(-1, 128) for block in blocks]
    used = sorted({kind for choices in kinds for kind in choices})
    right = [three[kind].reshape(-1, 256) for three in rights for kind in used]
    part = flat[0].shape[0] // steps
    whole = pl.BlockSpec(sums.shape, lambda s: (0,) * sums.ndim)
    return pl.pallas_call(
        functools.partial(gram_kernel, kinds, used, chunks),
        grid=(steps,),
        in_specs=[IN_SMEM]
        + [pl.BlockSpec((part, 128), lambda s: (s, 0))] * len(flat)
        + [pl.BlockSpec((part, 256), lambda s: (s, 0))] * len(right)
        + [whole]
        + [ANYWHERE] * len(after),
        out_specs=whole,
        out_shape=jax.ShapeDtypeStruct(sums.shape, jnp.float32),
        scratch_shapes=[pltpu.VMEM((len(kinds), 128 * chunks, 256 * chunks), jnp.float32)],
        compiler_params=pltpu.CompilerParams(vmem_limit_bytes=GRAM_LIMIT),
        cost_estimate=cost(len(flat) * flat[0].size * 8),
        name="gram",
    )(plan, *flat, *right, sums, *after)


def hop_operands(hop, up, down, low_a, low_b):
    bands = lax.axis_size("band")
    band = lax.axis_index("band")
    mid = bands // 2
    if hop == mid and mid > 1:
        up = jnp.where(band < mid - 1, low_b, up)
        down = jnp.where(band > bands - mid, low_a, down)
    return up, down


def behind(arrays, after):
    return pl.pallas_call(
        lambda *refs: None,
        in_specs=[ANYWHERE] * (len(arrays) + len(after)),
        out_specs=[ANYWHERE] * len(arrays),
        out_shape=[jax.ShapeDtypeStruct(x.shape, x.dtype) for x in arrays],
        input_output_aliases={i: i for i in range(len(arrays))},
        name="behind",
    )(*arrays, *after)


def hop_move(hop, up, down):
    bands = lax.axis_size("band")
    mid = bands // 2
    pairs = [b for b in range(hop, bands) if b - hop < mid]
    if hop >= mid:
        pairs = pairs + list(range(hop - mid + 1, mid))
    up = lax.ppermute(up, "band", [(b - 1, b) for b in pairs])
    down = lax.ppermute(down, "band", [(bands - b, bands - 1 - b) for b in pairs])
    return up, down


def hop_plan(hop, bands, band):
    mid = bands // 2
    late = hop - mid + 1
    skip = 3

    def one(place, main, other, sign):
        is_main = jnp.logical_and(place >= hop, place - hop < mid)
        is_late = jnp.logical_and(hop >= mid, jnp.logical_and(place >= late, place < mid))
        kind = jnp.where(is_main, main, jnp.where(is_late, other, skip))
        slot = band - sign * jnp.where(is_main, hop, jnp.where(is_late, late, 0))
        return [kind, slot]

    return one(band, 0, 1, 1) + one(bands - 1 - band, 2, 0, -1)


def summed_over_domain(table):
    count = lax.axis_size("domain")
    me = lax.axis_index("domain")
    bit = 1
    table = table.reshape(2, count, table.shape[1] // count, table.shape[2])
    while bit < count:
        groups = table.reshape((2, table.shape[1] // 2, 2) + table.shape[2:])
        mine = lax.rem(me // bit, 2)
        keep = lax.dynamic_index_in_dim(groups, mine, axis=2, keepdims=False)
        send = lax.dynamic_index_in_dim(groups, 1 - mine, axis=2, keepdims=False)
        table = keep + lax.ppermute(send, "domain", [(i, i ^ bit) for i in range(count)])
        bit *= 2
    return table[:, 0]


def other_triangle(table):
    bands, count = lax.axis_size("band"), lax.axis_size("domain")
    d, b = lax.axis_index("domain"), lax.axis_index("band")
    ratio = count // bands
    rows = table.shape[1]
    place = lax.rem(d, ratio)
    pieces = []
    for shift in range(ratio):
        to = lax.rem(place + shift, ratio)
        block = lax.dynamic_slice_in_dim(table, to * rows, rows, axis=2)
        pairs = []
        for i in range(count):
            for j in range(bands):
                target = ratio * j + (i % ratio + shift) % ratio
                pairs.append((i * bands + j, target * bands + i // ratio))
        pieces.append(lax.ppermute(block, ("domain", "band"), pairs).transpose(0, 2, 1))
    ordered = [
        lax.dynamic_index_in_dim(
            jnp.stack(pieces), lax.rem(place - t + ratio, ratio), axis=0, keepdims=False
        )
        for t in range(ratio)
    ]
    out = jnp.concatenate(ordered, axis=2)
    return jnp.where(d // ratio == b, 0.0, out)


def pot_kernel(diagonal, out):
    flipped = halves(jnp.broadcast_to(diagonal[0], (GROUP, diagonal.shape[2])))
    for y in range(out.shape[1]):
        out[0, y] = flipped[y * NZ : (y + 1) * NZ]


def spread(diagonal):
    nx, cells = diagonal.shape
    ny = cells // NZ // 2
    return pl.pallas_call(
        pot_kernel,
        grid=(nx,),
        in_specs=[pl.BlockSpec((1, 1, cells), lambda s: (s, 0, 0))],
        out_specs=pl.BlockSpec((1, ny, NZ, 128), lambda s: (s, 0, 0, 0)),
        out_shape=jax.ShapeDtypeStruct((nx, ny, NZ, 128), jnp.float32),
        compiler_params=pltpu.CompilerParams(vmem_limit_bytes=SMALL_LIMIT),
        cost_estimate=cost(128 * nx * cells * 5),
        name="spread",
    )(diagonal.reshape(nx, 1, cells))


def shards(orbitals, potential):
    own, nx, cells = orbitals.shape
    chunks = own // GROUP
    bands = lax.axis_size("band")
    total_cells = lax.axis_size("domain") * potential.size

    pot = spread((3.0 * kinetic * coeffs[0] + potential - center) / half_width)

    field = orbitals.transpose(1, 0, 2)
    packed = [pack(field, c) for c in range(chunks)]
    cur = [packed[c][0] for c in range(chunks)]
    edges = [(packed[c][1], packed[c][2]) for c in range(chunks)]
    token = packed[-1][0]
    prev = [None] * chunks
    lows = [None] * chunks
    for step in range(4):
        mode = "first" if step == 0 else ("last" if step == 3 else "middle")
        for c in range(chunks):
            below, above = exchange(*edges[c])
            after = [token]
            earlier = edges[0] if step == 3 and c > 0 else ()
            out = apply_op(mode, cur[c], prev[c], below, above, pot, after=after, earlier=earlier)
            prev[c], cur[c], edges[c] = cur[c], out[0], (out[1], out[2])
            lows[c] = out[3:5]
            token = out[0]
    band = lax.axis_index("band")
    lower = (band < bands // 2).astype(jnp.int32).reshape(1)
    ups, downs = [[] for _ in range(chunks)], [[] for _ in range(chunks)]
    sending, rights = [], []

    def move(c, hop):
        up, down = hop_move(hop, *sending[c])
        ups[c].append(up)
        downs[c].append(down)

    for c in range(chunks):
        sending.append(tuple(lows[c]))
        move(c, 1)
    halo = exchange(*edges[-1])
    for c in range(chunks):
        if bands > 2:
            sending[c] = hop_operands(2, ups[c][0], downs[c][0], *lows[c])
            move(c, 2)
        after = [token] if c > 0 else [token, ups[0][-1], downs[0][-1]]
        chunk = c if chunks > 1 else None
        rights.append(apply_op("image", cur[c], None, *halo, pot, lower, after, chunk=chunk))
        token = rights[-1][0]
    zeros = jnp.zeros((2, bands, chunks, GROUP, 128), jnp.float32)
    for hop in range(3, bands):
        for c in range(chunks):
            sending[c] = hop_operands(hop, ups[c][-1], downs[c][-1], *lows[c])
            if hop == 3 and c == chunks - 1:
                ups[c][-1], downs[c][-1], zeros = behind([*sending[c], zeros], [token])
                sending[c] = (ups[c][-1], downs[c][-1])
            move(c, hop)

    plans = [hop_plan(hop, bands, band) for hop in range(1, bands)]
    late = [0 <= hop - bands // 2 < bands // 2 - 1 for hop in range(1, bands)]
    kinds = [((0, 1), (2, 0)) if behind else ((0,), (2,)) for behind in late]

    def add_products(sums, first, last, after=()):
        blocks, plan, choice = [], [], []
        if first == 0:
            blocks = [lows[c][part] for part in range(2) for c in range(chunks)]
            choice = [(0,), (1,)]
            plan = [jnp.int32(0), band, jnp.int32(1), band]
        for i in range(max(first, 1) - 1, last):
            blocks += [ups[c][i] for c in range(chunks)] + [downs[c][i] for c in range(chunks)]
            plan = plan + plans[i]
            choice += kinds[i]
        rows = jnp.stack(plan).astype(jnp.int32)
        return gram(blocks, tuple(choice), rows, rights, sums, after=after)

    done = max(bands - 2, 1)
    table = zeros
    for last in range(1, done + 1):
        table = add_products(table, 0 if last == 1 else last, last)
    filtered = unpack(cur, own, after=[table])
    if bands > done + 1:
        table = add_products(table, bands - 1, bands - 1, [filtered])
    table = table.reshape(2, bands * own, 128)[:, :, :own]
    table = summed_over_domain(table)
    table = (table + other_triangle(table)) / total_cells
    return (filtered.transpose(1, 0, 2), table[0], table[1])


def solution(mesh):
    placed = (P("band", "domain", None), P("domain", None))
    return jax.shard_map(
        shards,
        mesh=mesh,
        in_specs=placed,
        out_specs=(P("band", "domain", None), P("domain", "band"), P("domain", "band")),
        check_vma=False,
    )
```

```python
import functools

import jax
import jax.numpy as jnp
from jax import lax
from jax.experimental import pallas as pl
from jax.experimental.pallas import tpu as pltpu
from jax.sharding import PartitionSpec as P

NZ = 144
GROUP = 64
TILE = 16
PAD = 8
CUT = 72
PART = 80
FIRST_B = NZ - PART
SMALL_LIMIT = 6 << 20
GRAM_LIMIT = 56 << 20

coeffs = (-205.0 / 72.0, 8.0 / 5.0, -1.0 / 5.0, 8.0 / 315.0, -1.0 / 560.0)
kinetic = -0.5 / 0.09
center = 68.0
half_width = 48.0
scaled_coeffs = [kinetic * c / half_width for c in coeffs]
carry = [coeffs[k] / coeffs[k + 1] for k in range(1, 4)]

limits = {"first": 12 << 20, "middle": 15 << 20, "last": 19 << 20, "image": 14 << 20}

IN_VMEM = pl.BlockSpec(memory_space=pltpu.VMEM)
ANYWHERE = pl.BlockSpec(memory_space=pl.ANY)
IN_SMEM = pl.BlockSpec(memory_space=pltpu.SMEM)


def cost(moved):
    return pl.CostEstimate(flops=0, bytes_accessed=moved, transcendentals=0)


def rounded_planes(planes):
    sent, error = [], None
    for i, plane in enumerate(planes):
        value = plane if error is None else plane + carry[i - 1] * error
        low = value.astype(jnp.bfloat16)
        error = value - low.astype(jnp.float32)
        sent.append(low)
    return sent


def halves(rows):
    half = rows.shape[1] // 2
    wide = -(-half // 128) * 128
    far = pltpu.roll(rows, half, 1)
    return jnp.concatenate([rows[:, :wide], far[:, :wide]], axis=0).T


def pack_kernel(field, packed, below, above, error):
    step = pl.program_id(0)
    flipped = halves(field[0])
    place = lax.rem(step, 4)
    factor = jnp.where(
        place == 0, 0.0, jnp.where(place == 1, carry[0], jnp.where(place == 2, carry[1], carry[2]))
    ).astype(jnp.float32)

    @pl.when(step == 0)
    def _():
        error[...] = jnp.zeros_like(error)

    for y in range(packed.shape[1]):
        value = flipped[y * NZ : (y + 1) * NZ]
        packed[0, y, 0:PAD, :] = jnp.zeros((PAD, 128), jnp.float32)
        packed[0, y, NZ + PAD : NZ + 2 * PAD, :] = jnp.zeros((PAD, 128), jnp.float32)
        packed[0, y, PAD : NZ + PAD, :] = value

        @pl.when(step < 8)
        def _():
            wide = value + factor * error[y]
            low = wide.astype(jnp.bfloat16)
            error[y] = wide - low.astype(jnp.float32)

            @pl.when(step < 4)
            def _():
                below[step, y] = low

            @pl.when(step >= 4)
            def _():
                above[7 - step, y] = low


def pack(field, chunk):
    nx, _, cells = field.shape
    ny = cells // NZ // 2

    def plane(s):
        return jnp.where(s < 4, s, jnp.where(s < 8, nx + 3 - s, s - 4))

    edge = jax.ShapeDtypeStruct((4, ny, NZ, 128), jnp.bfloat16)
    edge_spec = pl.BlockSpec((4, ny, NZ, 128), lambda s: (0, 0, 0, 0))
    return pl.pallas_call(
        pack_kernel,
        grid=(nx,),
        in_specs=[pl.BlockSpec((1, GROUP, cells), lambda s: (plane(s), chunk, 0))],
        out_specs=[
            pl.BlockSpec((1, ny, NZ + 2 * PAD, 128), lambda s: (plane(s), 0, 0, 0)),
            edge_spec,
            edge_spec,
        ],
        out_shape=[jax.ShapeDtypeStruct((nx, ny, NZ + 2 * PAD, 128), jnp.float32), edge, edge],
        scratch_shapes=[pltpu.VMEM((ny, NZ, 128), jnp.float32)],
        compiler_params=pltpu.CompilerParams(vmem_limit_bytes=SMALL_LIMIT),
        cost_estimate=cost(2 * GROUP * nx * cells * 8),
        name="pack",
    )(field)


def unpack_kernel(rows, count, *refs):
    chunks, out = refs[:count], refs[-1]
    ny = chunks[0].shape[1]
    left = lax.broadcasted_iota(jnp.int32, (NZ, 128), 1) < GROUP
    near, far = [], []
    for y in range(ny):
        parts = [chunk[0, y, PAD : NZ + PAD, :] for chunk in chunks]
        if len(parts) == 1:
            near.append(parts[0])
            far.append(pltpu.roll(parts[0], GROUP, 1))
        else:
            near.append(jnp.where(left, parts[0], pltpu.roll(parts[1], GROUP, 1)))
            far.append(jnp.where(left, pltpu.roll(parts[0], GROUP, 1), parts[1]))
    out[0] = jnp.concatenate(near + far, axis=0).T[:rows]


def unpack(chunks, rows, after=()):
    nx, ny, depth, _ = chunks[0].shape
    cells = 2 * ny * NZ
    return pl.pallas_call(
        functools.partial(unpack_kernel, rows, len(chunks)),
        grid=(nx,),
        in_specs=[pl.BlockSpec((1, ny, depth, 128), lambda s: (s, 0, 0, 0))] * len(chunks)
        + [ANYWHERE] * len(after),
        out_specs=pl.BlockSpec((1, rows, cells), lambda s: (s, 0, 0)),
        out_shape=jax.ShapeDtypeStruct((nx, rows, cells), jnp.float32),
        compiler_params=pltpu.CompilerParams(vmem_limit_bytes=SMALL_LIMIT),
        cost_estimate=cost(rows * nx * cells * 16),
        name="unpack",
    )(*chunks, *after)


def apply_kernel(mode, waits, earlier, chunk, *refs):
    refs = list(refs)
    copies = []
    if earlier:
        sems = refs.pop()
    lower = refs.pop(0) if mode == "image" else None
    cur = refs.pop(0)
    prev = refs.pop(0) if mode in ("middle", "last") else None
    below, above, pot = refs.pop(0), refs.pop(0), refs.pop(0)
    if chunk is not None:
        below, above = below.at[chunk], above.at[chunk]
    refs = refs[waits:]
    if earlier:
        copies = [pltpu.make_async_copy(refs[i], refs[3 + i].at[0], sems.at[i]) for i in range(2)]
        refs = refs[2:]
        refs[1:3] = [refs[1].at[1], refs[2].at[1]]
    for copy in copies:
        copy.start()
    nx, ny = cur.shape[:2]
    left = lax.broadcasted_iota(jnp.int32, (TILE, 128), 1) < GROUP
    if mode == "image":
        part_a, part_b, part_w = refs
    else:
        new, out_below, out_above = refs[:3]
        zero = jnp.zeros((PAD, 128), jnp.float32)
        for x in range(nx):
            for y in range(ny):
                new[x, y, 0:PAD, :] = zero
                new[x, y, NZ + PAD : NZ + 2 * PAD, :] = zero

    def body(t, in_a, in_b):
        z = pl.multiple_of(t * TILE, TILE)
        in_cut = lax.broadcasted_iota(jnp.int32, (TILE, 128), 0) + FIRST_B >= CUT

        def plane(x, y):
            if x < 0:
                return below[4 + x, y, pl.ds(z, TILE), :].astype(jnp.float32)
            if x >= nx:
                return above[x - nx, y, pl.ds(z, TILE), :].astype(jnp.float32)
            return cur[x, y, pl.ds(z + PAD, TILE), :]

        results = []
        for x in range(nx):
            mine = [plane(x, y) for y in range(ny)]
            other = [pltpu.roll(a, GROUP, 1) for a in mine]
            after = [jnp.where(left, a, 0.0) for a in other]
            before = [jnp.where(left, 0.0, a) for a in other]
            row = []
            for y in range(ny):
                total = pot[x, y, pl.ds(z, TILE), :] * mine[y]
                both = in_a and in_b and mode == "image"
                strip = jnp.zeros_like(total) if both else None
                for k in range(1, 5):
                    pairs = plane(x - k, y) + plane(x + k, y)
                    if k == ny:
                        pairs = pairs + other[y]
                    else:
                        up = mine[y + k] if y + k < ny else after[y + k - ny]
                        down = mine[y - k] if y >= k else before[y - k + ny]
                        pairs = pairs + (up + down)
                    forth = cur[x, y, pl.ds(z + PAD + k, TILE), :]
                    back = cur[x, y, pl.ds(z + PAD - k, TILE), :]
                    if both:
                        depth = lax.broadcasted_iota(jnp.int32, (TILE, 128), 0) + FIRST_B
                        cut = jnp.where(in_cut, pairs, 0.0) + jnp.where(depth + k >= CUT, forth, 0.0)
                        cut = cut + jnp.where(depth - k >= CUT, back, 0.0)
                        strip = strip + scaled_coeffs[k] * cut
                        if k == 1:
                            strip = strip + jnp.where(in_cut, total, 0.0)
                    pairs = pairs + (forth + back)
                    total = total + scaled_coeffs[k] * pairs
                if mode == "image":
                    low = mine[y].astype(jnp.bfloat16)
                    image = total.astype(jnp.bfloat16)
                    if both:
                        none = jnp.zeros_like(low)
                        keep_b = in_cut.astype(jnp.float32).astype(jnp.bfloat16)
                        keep_a = 1.0 - keep_b
                        part_a[x, y, pl.ds(z, TILE), 0:128] = image * keep_a
                        part_a[x, y, pl.ds(z, TILE), 128:256] = low * keep_a
                        part_b[x, y, 0:TILE, 0:128] = image * keep_b
                        part_b[x, y, 0:TILE, 128:256] = low * keep_b
                        whole = jnp.where(in_cut, total, 0.0)
                        chosen = jnp.where(lower[0] > 0, strip, whole).astype(jnp.bfloat16)
                        part_w[x, y, 0:TILE, 0:128] = chosen
                        part_w[x, y, 0:TILE, 128:256] = low * keep_b
                    elif in_a:
                        part_a[x, y, pl.ds(z, TILE), 0:128] = image
                        part_a[x, y, pl.ds(z, TILE), 128:256] = low
                    else:
                        for part in (part_b, part_w):
                            part[x, y, pl.ds(z - FIRST_B, TILE), 0:128] = image
                            part[x, y, pl.ds(z - FIRST_B, TILE), 128:256] = low
                    continue
                if prev is not None:
                    total = (total + total) - prev[x, y, pl.ds(z + PAD, TILE), :]
                new[x, y, pl.ds(z + PAD, TILE), :] = total
                if mode == "last":
                    low = total.astype(jnp.bfloat16)
                    if in_a:
                        refs[3][x, y, pl.ds(z, TILE), :] = low
                    if in_b:
                        refs[4][x, y, pl.ds(z - FIRST_B, TILE), :] = low
                row.append(total)
            results.append(row)
        if mode == "image":
            return
        for y in range(ny):
            for i, low in enumerate(rounded_planes([results[i][y] for i in range(4)])):
                out_below[i, y, pl.ds(z, TILE), :] = low
            for i, low in enumerate(rounded_planes([results[nx - 1 - i][y] for i in range(4)])):
                out_above[3 - i, y, pl.ds(z, TILE), :] = low

    def loop(start, stop, in_a, in_b):
        def step(t, _):
            body(t, in_a, in_b)
            return 0

        lax.fori_loop(start, stop, step, 0)

    if mode in ("first", "middle"):
        loop(0, NZ // TILE, False, False)
    else:
        loop(0, FIRST_B // TILE, True, False)
        loop(FIRST_B // TILE, PART // TILE, True, True)
        loop(PART // TILE, NZ // TILE, False, True)
    for copy in copies:
        copy.wait()


def apply_op(mode, cur, prev, below, above, pot, lower=None, after=(), earlier=(), chunk=None):
    nx, ny = cur.shape[:2]
    edge = jax.ShapeDtypeStruct(((2,) if earlier else ()) + (4, ny, NZ, 128), jnp.bfloat16)
    part = jax.ShapeDtypeStruct((nx, ny, PART, 128), jnp.bfloat16)
    wide = jax.ShapeDtypeStruct((nx, ny, PART, 256), jnp.bfloat16)
    shapes = [jax.ShapeDtypeStruct(cur.shape, cur.dtype), edge, edge]
    if mode == "last":
        shapes = shapes + [part, part]
    if mode == "image":
        shapes = [wide, wide, wide]
    args = [cur] + ([prev] if prev is not None else []) + [below, above, pot]
    specs = [IN_VMEM] * len(args)
    if mode == "image":
        args, specs = [lower] + args, [IN_SMEM] + specs
    args = args + list(after) + list(earlier)
    specs = specs + [ANYWHERE] * (len(after) + len(earlier))
    return pl.pallas_call(
        functools.partial(apply_kernel, mode, len(after), bool(earlier), chunk),
        in_specs=specs,
        out_specs=[IN_VMEM] * len(shapes),
        out_shape=shapes,
        scratch_shapes=[pltpu.SemaphoreType.DMA((2,))] if earlier else [],
        compiler_params=pltpu.CompilerParams(vmem_limit_bytes=limits[mode]),
        cost_estimate=cost(22 * cur.size),
        name="apply_" + mode,
    )(*args)


def exchange(below, above):
    count = lax.axis_size("domain")
    up = [(i, i + 1) for i in range(count - 1)]
    down = [(i + 1, i) for i in range(count - 1)]
    return lax.ppermute(above, "domain", up), lax.ppermute(below, "domain", down)


def gram_kernel(kinds, used, chunks, plan, *refs):
    count = len(kinds)
    blocks, refs = refs[: count * chunks], refs[count * chunks :]
    rights, refs = refs[: len(used) * chunks], refs[len(used) * chunks :]
    sums, out, full = refs[0], refs[-2], refs[-1]
    left = lax.broadcasted_iota(jnp.int32, (GROUP, 128), 1) < GROUP
    step = pl.program_id(0)

    for i, choices in enumerate(kinds):
        for kind in choices:

            @pl.when(plan[2 * i] == kind)
            def _():
                mine = blocks[chunks * i : chunks * (i + 1)]
                turned = jnp.concatenate([block[...].T for block in mine], axis=0)
                ours = [rights[len(used) * c + used.index(kind)][...] for c in range(chunks)]
                value = jnp.dot(
                    turned, jnp.concatenate(ours, axis=1), preferred_element_type=jnp.float32
                )

                @pl.when(step == 0)
                def _():
                    full[i] = value

                @pl.when(step > 0)
                def _():
                    full[i] += value

    @pl.when(step == pl.num_programs(0) - 1)
    def _():
        out[...] = sums[...]
        for i in range(count):

            @pl.when(plan[2 * i] < 3)
            def _():
                for other in range(chunks):
                    top = slice(128 * other, 128 * other + GROUP)
                    low = slice(128 * other + GROUP, 128 * (other + 1))
                    for m in range(2):
                        lanes = slice(128 * m, 128 * (m + 1))
                        value = full[i, top, lanes] + pltpu.roll(full[i, low, lanes], GROUP, 1)
                        if chunks == 2:
                            lanes = slice(256 + 128 * m, 256 + 128 * (m + 1))
                            second = pltpu.roll(full[i, top, lanes], GROUP, 1)
                            value = jnp.where(left, value, second + full[i, low, lanes])
                        out[m, plan[2 * i + 1], other] += value


def gram(blocks, kinds, plan, rights, sums, after=()):
    chunks = len(rights)
    steps = 3
    flat = [block.reshape(-1, 128) for block in blocks]
    used = sorted({kind for choices in kinds for kind in choices})
    right = [three[kind].reshape(-1, 256) for three in rights for kind in used]
    part = flat[0].shape[0] // steps
    whole = pl.BlockSpec(sums.shape, lambda s: (0,) * sums.ndim)
    return pl.pallas_call(
        functools.partial(gram_kernel, kinds, used, chunks),
        grid=(steps,),
        in_specs=[IN_SMEM]
        + [pl.BlockSpec((part, 128), lambda s: (s, 0))] * len(flat)
        + [pl.BlockSpec((part, 256), lambda s: (s, 0))] * len(right)
        + [whole]
        + [ANYWHERE] * len(after),
        out_specs=whole,
        out_shape=jax.ShapeDtypeStruct(sums.shape, jnp.float32),
        scratch_shapes=[pltpu.VMEM((len(kinds), 128 * chunks, 256 * chunks), jnp.float32)],
        compiler_params=pltpu.CompilerParams(vmem_limit_bytes=GRAM_LIMIT),
        cost_estimate=cost(len(flat) * flat[0].size * 8),
        name="gram",
    )(plan, *flat, *right, sums, *after)


def hop_operands(hop, up, down, low_a, low_b):
    bands = lax.axis_size("band")
    band = lax.axis_index("band")
    mid = bands // 2
    if hop == mid and mid > 1:
        up = jnp.where(band < mid - 1, low_b, up)
        down = jnp.where(band > bands - mid, low_a, down)
    return up, down


def behind(arrays, after):
    return pl.pallas_call(
        lambda *refs: None,
        in_specs=[ANYWHERE] * (len(arrays) + len(after)),
        out_specs=[ANYWHERE] * len(arrays),
        out_shape=[jax.ShapeDtypeStruct(x.shape, x.dtype) for x in arrays],
        input_output_aliases={i: i for i in range(len(arrays))},
        name="behind",
    )(*arrays, *after)


def hop_move(hop, up, down):
    bands = lax.axis_size("band")
    mid = bands // 2
    pairs = [b for b in range(hop, bands) if b - hop < mid]
    if hop >= mid:
        pairs = pairs + list(range(hop - mid + 1, mid))
    up = lax.ppermute(up, "band", [(b - 1, b) for b in pairs])
    down = lax.ppermute(down, "band", [(bands - b, bands - 1 - b) for b in pairs])
    return up, down


def hop_plan(hop, bands, band):
    mid = bands // 2
    late = hop - mid + 1
    skip = 3

    def one(place, main, other, sign):
        is_main = jnp.logical_and(place >= hop, place - hop < mid)
        is_late = jnp.logical_and(hop >= mid, jnp.logical_and(place >= late, place < mid))
        kind = jnp.where(is_main, main, jnp.where(is_late, other, skip))
        slot = band - sign * jnp.where(is_main, hop, jnp.where(is_late, late, 0))
        return [kind, slot]

    return one(band, 0, 1, 1) + one(bands - 1 - band, 2, 0, -1)


def summed_over_domain(table):
    count = lax.axis_size("domain")
    me = lax.axis_index("domain")
    table = table.reshape(2, count // 2, 2, table.shape[1] // count, table.shape[2])
    mine = lax.rem(me, 2)
    keep = lax.dynamic_index_in_dim(table, mine, axis=2, keepdims=False)
    send = lax.dynamic_index_in_dim(table, 1 - mine, axis=2, keepdims=False)
    table = keep + lax.ppermute(send, "domain", [(i, i ^ 1) for i in range(count)])
    total = lax.dynamic_index_in_dim(table, me // 2, axis=1, keepdims=False)
    for other in range(1, count // 2):
        send = lax.dynamic_index_in_dim(table, (me // 2) ^ other, axis=1, keepdims=False)
        pairs = [(i, i ^ (2 * other)) for i in range(count)]
        total = total + lax.ppermute(send, "domain", pairs)
    return total


def other_triangle(table):
    bands, count = lax.axis_size("band"), lax.axis_size("domain")
    d, b = lax.axis_index("domain"), lax.axis_index("band")
    ratio = count // bands
    rows = table.shape[1]
    place = lax.rem(d, ratio)
    pieces = []
    for shift in range(ratio):
        to = lax.rem(place + shift, ratio)
        block = lax.dynamic_slice_in_dim(table, to * rows, rows, axis=2)
        pairs = []
        for i in range(count):
            for j in range(bands):
                target = ratio * j + (i % ratio + shift) % ratio
                pairs.append((i * bands + j, target * bands + i // ratio))
        pieces.append(lax.ppermute(block, ("domain", "band"), pairs).transpose(0, 2, 1))
    ordered = [
        lax.dynamic_index_in_dim(
            jnp.stack(pieces), lax.rem(place - t + ratio, ratio), axis=0, keepdims=False
        )
        for t in range(ratio)
    ]
    out = jnp.concatenate(ordered, axis=2)
    return jnp.where(d // ratio == b, 0.0, out)


def pot_kernel(diagonal, out):
    flipped = halves(jnp.broadcast_to(diagonal[0], (GROUP, diagonal.shape[2])))
    for y in range(out.shape[1]):
        out[0, y] = flipped[y * NZ : (y + 1) * NZ]


def spread(diagonal):
    nx, cells = diagonal.shape
    ny = cells // NZ // 2
    return pl.pallas_call(
        pot_kernel,
        grid=(nx,),
        in_specs=[pl.BlockSpec((1, 1, cells), lambda s: (s, 0, 0))],
        out_specs=pl.BlockSpec((1, ny, NZ, 128), lambda s: (s, 0, 0, 0)),
        out_shape=jax.ShapeDtypeStruct((nx, ny, NZ, 128), jnp.float32),
        compiler_params=pltpu.CompilerParams(vmem_limit_bytes=SMALL_LIMIT),
        cost_estimate=cost(128 * nx * cells * 5),
        name="spread",
    )(diagonal.reshape(nx, 1, cells))


def shards(orbitals, potential):
    own, nx, cells = orbitals.shape
    chunks = own // GROUP
    bands = lax.axis_size("band")
    total_cells = lax.axis_size("domain") * potential.size

    pot = spread((3.0 * kinetic * coeffs[0] + potential - center) / half_width)

    field = orbitals.transpose(1, 0, 2)
    packed = [pack(field, c) for c in range(chunks)]
    cur = [packed[c][0] for c in range(chunks)]
    edges = [(packed[c][1], packed[c][2]) for c in range(chunks)]
    token = packed[-1][0]
    prev = [None] * chunks
    lows = [None] * chunks
    for step in range(4):
        mode = "first" if step == 0 else ("last" if step == 3 else "middle")
        for c in range(chunks):
            below, above = exchange(*edges[c])
            after = [token]
            earlier = edges[0] if step == 3 and c > 0 else ()
            out = apply_op(mode, cur[c], prev[c], below, above, pot, after=after, earlier=earlier)
            prev[c], cur[c], edges[c] = cur[c], out[0], (out[1], out[2])
            lows[c] = out[3:5]
            token = out[0]
    band = lax.axis_index("band")
    lower = (band < bands // 2).astype(jnp.int32).reshape(1)
    ups, downs = [[] for _ in range(chunks)], [[] for _ in range(chunks)]
    sending, rights = [], []

    def move(c, hop):
        up, down = hop_move(hop, *sending[c])
        ups[c].append(up)
        downs[c].append(down)

    for c in range(chunks):
        sending.append(tuple(lows[c]))
        move(c, 1)
    halo = exchange(*edges[-1])
    for c in range(chunks):
        if bands > 2:
            sending[c] = hop_operands(2, ups[c][0], downs[c][0], *lows[c])
            move(c, 2)
        after = [token] if c > 0 else [token, ups[0][-1], downs[0][-1]]
        chunk = c if chunks > 1 else None
        rights.append(apply_op("image", cur[c], None, *halo, pot, lower, after, chunk=chunk))
        token = rights[-1][0]
    zeros = jnp.zeros((2, bands, chunks, GROUP, 128), jnp.float32)
    for hop in range(3, bands):
        for c in range(chunks):
            sending[c] = hop_operands(hop, ups[c][-1], downs[c][-1], *lows[c])
            if hop == 3 and c == chunks - 1:
                ups[c][-1], downs[c][-1], zeros = behind([*sending[c], zeros], [token])
                sending[c] = (ups[c][-1], downs[c][-1])
            move(c, hop)

    plans = [hop_plan(hop, bands, band) for hop in range(1, bands)]
    late = [0 <= hop - bands // 2 < bands // 2 - 1 for hop in range(1, bands)]
    kinds = [((0, 1), (2, 0)) if behind else ((0,), (2,)) for behind in late]

    def add_products(sums, first, last, after=()):
        blocks, plan, choice = [], [], []
        if first == 0:
            blocks = [lows[c][part] for part in range(2) for c in range(chunks)]
            choice = [(0,), (1,)]
            plan = [jnp.int32(0), band, jnp.int32(1), band]
        for i in range(max(first, 1) - 1, last):
            blocks += [ups[c][i] for c in range(chunks)] + [downs[c][i] for c in range(chunks)]
            plan = plan + plans[i]
            choice += kinds[i]
        rows = jnp.stack(plan).astype(jnp.int32)
        return gram(blocks, tuple(choice), rows, rights, sums, after=after)

    done = max(bands - 2, 1)
    table = zeros
    for last in range(1, done + 1):
        table = add_products(table, 0 if last == 1 else last, last)
    filtered = unpack(cur, own, after=[table])
    if bands > done + 1:
        table = add_products(table, bands - 1, bands - 1, [filtered])
    table = table.reshape(2, bands * own, 128)[:, :, :own]
    table = summed_over_domain(table)
    table = (table + other_triangle(table)) / total_cells
    return (filtered.transpose(1, 0, 2), table[0], table[1])


def solution(mesh):
    placed = (P("band", "domain", None), P("domain", None))
    return jax.shard_map(
        shards,
        mesh=mesh,
        in_specs=placed,
        out_specs=(P("band", "domain", None), P("domain", "band"), P("domain", "band")),
        check_vma=False,
    )
```

```python
import functools

import jax
import jax.numpy as jnp
from jax import lax
from jax.experimental import pallas as pl
from jax.experimental.pallas import tpu as pltpu
from jax.sharding import PartitionSpec as P

NZ = 144
GROUP = 64
TILE = 16
PAD = 8
CUT = 72
PART = 80
FIRST_B = NZ - PART
SMALL_LIMIT = 6 << 20
GRAM_LIMIT = 56 << 20
LAST_GRAM_LIMIT = 20 << 20

coeffs = (-205.0 / 72.0, 8.0 / 5.0, -1.0 / 5.0, 8.0 / 315.0, -1.0 / 560.0)
kinetic = -0.5 / 0.09
center = 68.0
half_width = 48.0
scaled_coeffs = [kinetic * c / half_width for c in coeffs]
carry = [coeffs[k] / coeffs[k + 1] for k in range(1, 4)]

limits = {"first": 12 << 20, "middle": 15 << 20, "last": 19 << 20, "image": 14 << 20}

IN_VMEM = pl.BlockSpec(memory_space=pltpu.VMEM)
ANYWHERE = pl.BlockSpec(memory_space=pl.ANY)
IN_SMEM = pl.BlockSpec(memory_space=pltpu.SMEM)


def cost(moved):
    return pl.CostEstimate(flops=0, bytes_accessed=moved, transcendentals=0)


def rounded_planes(planes):
    sent, error = [], None
    for i, plane in enumerate(planes):
        value = plane if error is None else plane + carry[i - 1] * error
        low = value.astype(jnp.bfloat16)
        error = value - low.astype(jnp.float32)
        sent.append(low)
    return sent


def halves(rows):
    half = rows.shape[1] // 2
    wide = -(-half // 128) * 128
    far = pltpu.roll(rows, half, 1)
    return jnp.concatenate([rows[:, :wide], far[:, :wide]], axis=0).T


def pack_kernel(field, packed, below, above, error):
    step = pl.program_id(0)
    flipped = halves(field[0])
    place = lax.rem(step, 4)
    factor = jnp.where(
        place == 0, 0.0, jnp.where(place == 1, carry[0], jnp.where(place == 2, carry[1], carry[2]))
    ).astype(jnp.float32)

    @pl.when(step == 0)
    def _():
        error[...] = jnp.zeros_like(error)

    for y in range(packed.shape[1]):
        value = flipped[y * NZ : (y + 1) * NZ]
        packed[0, y, 0:PAD, :] = jnp.zeros((PAD, 128), jnp.float32)
        packed[0, y, NZ + PAD : NZ + 2 * PAD, :] = jnp.zeros((PAD, 128), jnp.float32)
        packed[0, y, PAD : NZ + PAD, :] = value

        @pl.when(step < 8)
        def _():
            wide = value + factor * error[y]
            low = wide.astype(jnp.bfloat16)
            error[y] = wide - low.astype(jnp.float32)

            @pl.when(step < 4)
            def _():
                below[step, y] = low

            @pl.when(step >= 4)
            def _():
                above[7 - step, y] = low


def pack(field, chunk):
    nx, _, cells = field.shape
    ny = cells // NZ // 2

    def plane(s):
        return jnp.where(s < 4, s, jnp.where(s < 8, nx + 3 - s, s - 4))

    edge = jax.ShapeDtypeStruct((4, ny, NZ, 128), jnp.bfloat16)
    edge_spec = pl.BlockSpec((4, ny, NZ, 128), lambda s: (0, 0, 0, 0))
    return pl.pallas_call(
        pack_kernel,
        grid=(nx,),
        in_specs=[pl.BlockSpec((1, GROUP, cells), lambda s: (plane(s), chunk, 0))],
        out_specs=[
            pl.BlockSpec((1, ny, NZ + 2 * PAD, 128), lambda s: (plane(s), 0, 0, 0)),
            edge_spec,
            edge_spec,
        ],
        out_shape=[jax.ShapeDtypeStruct((nx, ny, NZ + 2 * PAD, 128), jnp.float32), edge, edge],
        scratch_shapes=[pltpu.VMEM((ny, NZ, 128), jnp.float32)],
        compiler_params=pltpu.CompilerParams(vmem_limit_bytes=SMALL_LIMIT),
        cost_estimate=cost(2 * GROUP * nx * cells * 8),
        name="pack",
    )(field)


def unpack_kernel(rows, count, *refs):
    chunks, out = refs[:count], refs[-1]
    ny = chunks[0].shape[1]
    left = lax.broadcasted_iota(jnp.int32, (NZ, 128), 1) < GROUP
    near, far = [], []
    for y in range(ny):
        parts = [chunk[0, y, PAD : NZ + PAD, :] for chunk in chunks]
        if len(parts) == 1:
            near.append(parts[0])
            far.append(pltpu.roll(parts[0], GROUP, 1))
        else:
            near.append(jnp.where(left, parts[0], pltpu.roll(parts[1], GROUP, 1)))
            far.append(jnp.where(left, pltpu.roll(parts[0], GROUP, 1), parts[1]))
    out[0] = jnp.concatenate(near + far, axis=0).T[:rows]


def unpack(chunks, rows, after=()):
    nx, ny, depth, _ = chunks[0].shape
    cells = 2 * ny * NZ
    return pl.pallas_call(
        functools.partial(unpack_kernel, rows, len(chunks)),
        grid=(nx,),
        in_specs=[pl.BlockSpec((1, ny, depth, 128), lambda s: (s, 0, 0, 0))] * len(chunks)
        + [ANYWHERE] * len(after),
        out_specs=pl.BlockSpec((1, rows, cells), lambda s: (s, 0, 0)),
        out_shape=jax.ShapeDtypeStruct((nx, rows, cells), jnp.float32),
        compiler_params=pltpu.CompilerParams(vmem_limit_bytes=SMALL_LIMIT),
        cost_estimate=cost(rows * nx * cells * 16),
        name="unpack",
    )(*chunks, *after)


def apply_kernel(mode, waits, earlier, chunk, *refs):
    refs = list(refs)
    copies = []
    if earlier:
        sems = refs.pop()
    lower = refs.pop(0) if mode == "image" else None
    cur = refs.pop(0)
    prev = refs.pop(0) if mode in ("middle", "last") else None
    below, above, pot = refs.pop(0), refs.pop(0), refs.pop(0)
    if chunk is not None:
        below, above = below.at[chunk], above.at[chunk]
    refs = refs[waits:]
    if earlier:
        copies = [pltpu.make_async_copy(refs[i], refs[3 + i].at[0], sems.at[i]) for i in range(2)]
        refs = refs[2:]
        refs[1:3] = [refs[1].at[1], refs[2].at[1]]
    for copy in copies:
        copy.start()
    nx, ny = cur.shape[:2]
    left = lax.broadcasted_iota(jnp.int32, (TILE, 128), 1) < GROUP
    if mode == "image":
        part_a, part_b, part_w = refs
    else:
        new, out_below, out_above = refs[:3]
        zero = jnp.zeros((PAD, 128), jnp.float32)
        for x in range(nx):
            for y in range(ny):
                new[x, y, 0:PAD, :] = zero
                new[x, y, NZ + PAD : NZ + 2 * PAD, :] = zero

    def body(t, in_a, in_b):
        z = pl.multiple_of(t * TILE, TILE)
        in_cut = lax.broadcasted_iota(jnp.int32, (TILE, 128), 0) + FIRST_B >= CUT

        def plane(x, y):
            if x < 0:
                return below[4 + x, y, pl.ds(z, TILE), :].astype(jnp.float32)
            if x >= nx:
                return above[x - nx, y, pl.ds(z, TILE), :].astype(jnp.float32)
            return cur[x, y, pl.ds(z + PAD, TILE), :]

        results = []
        for x in range(nx):
            mine = [plane(x, y) for y in range(ny)]
            other = [pltpu.roll(a, GROUP, 1) for a in mine]
            after = [jnp.where(left, a, 0.0) for a in other]
            before = [jnp.where(left, 0.0, a) for a in other]
            row = []
            for y in range(ny):
                total = pot[x, y, pl.ds(z, TILE), :] * mine[y]
                both = in_a and in_b and mode == "image"
                strip = jnp.zeros_like(total) if both else None
                for k in range(1, 5):
                    pairs = plane(x - k, y) + plane(x + k, y)
                    if k == ny:
                        pairs = pairs + other[y]
                    else:
                        up = mine[y + k] if y + k < ny else after[y + k - ny]
                        down = mine[y - k] if y >= k else before[y - k + ny]
                        pairs = pairs + (up + down)
                    forth = cur[x, y, pl.ds(z + PAD + k, TILE), :]
                    back = cur[x, y, pl.ds(z + PAD - k, TILE), :]
                    if both:
                        depth = lax.broadcasted_iota(jnp.int32, (TILE, 128), 0) + FIRST_B
                        cut = jnp.where(in_cut, pairs, 0.0) + jnp.where(depth + k >= CUT, forth, 0.0)
                        cut = cut + jnp.where(depth - k >= CUT, back, 0.0)
                        strip = strip + scaled_coeffs[k] * cut
                        if k == 1:
                            strip = strip + jnp.where(in_cut, total, 0.0)
                    pairs = pairs + (forth + back)
                    total = total + scaled_coeffs[k] * pairs
                if mode == "image":
                    low = mine[y].astype(jnp.bfloat16)
                    image = total.astype(jnp.bfloat16)
                    if both:
                        none = jnp.zeros_like(low)
                        keep_b = in_cut.astype(jnp.float32).astype(jnp.bfloat16)
                        keep_a = 1.0 - keep_b
                        part_a[x, y, pl.ds(z, TILE), 0:128] = image * keep_a
                        part_a[x, y, pl.ds(z, TILE), 128:256] = low * keep_a
                        part_b[x, y, 0:TILE, 0:128] = image * keep_b
                        part_b[x, y, 0:TILE, 128:256] = low * keep_b
                        whole = jnp.where(in_cut, total, 0.0)
                        chosen = jnp.where(lower[0] > 0, strip, whole).astype(jnp.bfloat16)
                        part_w[x, y, 0:TILE, 0:128] = chosen
                        part_w[x, y, 0:TILE, 128:256] = low * keep_b
                    elif in_a:
                        part_a[x, y, pl.ds(z, TILE), 0:128] = image
                        part_a[x, y, pl.ds(z, TILE), 128:256] = low
                    else:
                        for part in (part_b, part_w):
                            part[x, y, pl.ds(z - FIRST_B, TILE), 0:128] = image
                            part[x, y, pl.ds(z - FIRST_B, TILE), 128:256] = low
                    continue
                if prev is not None:
                    total = (total + total) - prev[x, y, pl.ds(z + PAD, TILE), :]
                new[x, y, pl.ds(z + PAD, TILE), :] = total
                if mode == "last":
                    low = total.astype(jnp.bfloat16)
                    if in_a:
                        refs[3][x, y, pl.ds(z, TILE), :] = low
                    if in_b:
                        refs[4][x, y, pl.ds(z - FIRST_B, TILE), :] = low
                row.append(total)
            results.append(row)
        if mode == "image":
            return
        for y in range(ny):
            for i, low in enumerate(rounded_planes([results[i][y] for i in range(4)])):
                out_below[i, y, pl.ds(z, TILE), :] = low
            for i, low in enumerate(rounded_planes([results[nx - 1 - i][y] for i in range(4)])):
                out_above[3 - i, y, pl.ds(z, TILE), :] = low

    def loop(start, stop, in_a, in_b):
        def step(t, _):
            body(t, in_a, in_b)
            return 0

        lax.fori_loop(start, stop, step, 0)

    if mode in ("first", "middle"):
        loop(0, NZ // TILE, False, False)
    else:
        loop(0, FIRST_B // TILE, True, False)
        loop(FIRST_B // TILE, PART // TILE, True, True)
        loop(PART // TILE, NZ // TILE, False, True)
    for copy in copies:
        copy.wait()


def apply_op(mode, cur, prev, below, above, pot, lower=None, after=(), earlier=(), chunk=None):
    nx, ny = cur.shape[:2]
    edge = jax.ShapeDtypeStruct(((2,) if earlier else ()) + (4, ny, NZ, 128), jnp.bfloat16)
    part = jax.ShapeDtypeStruct((nx, ny, PART, 128), jnp.bfloat16)
    wide = jax.ShapeDtypeStruct((nx, ny, PART, 256), jnp.bfloat16)
    shapes = [jax.ShapeDtypeStruct(cur.shape, cur.dtype), edge, edge]
    if mode == "last":
        shapes = shapes + [part, part]
    if mode == "image":
        shapes = [wide, wide, wide]
    args = [cur] + ([prev] if prev is not None else []) + [below, above, pot]
    specs = [IN_VMEM] * len(args)
    if mode == "image":
        args, specs = [lower] + args, [IN_SMEM] + specs
    args = args + list(after) + list(earlier)
    specs = specs + [ANYWHERE] * (len(after) + len(earlier))
    return pl.pallas_call(
        functools.partial(apply_kernel, mode, len(after), bool(earlier), chunk),
        in_specs=specs,
        out_specs=[IN_VMEM] * len(shapes),
        out_shape=shapes,
        scratch_shapes=[pltpu.SemaphoreType.DMA((2,))] if earlier else [],
        compiler_params=pltpu.CompilerParams(vmem_limit_bytes=limits[mode]),
        cost_estimate=cost(22 * cur.size),
        name="apply_" + mode,
    )(*args)


def exchange(below, above):
    count = lax.axis_size("domain")
    up = [(i, i + 1) for i in range(count - 1)]
    down = [(i + 1, i) for i in range(count - 1)]
    return lax.ppermute(above, "domain", up), lax.ppermute(below, "domain", down)


def gram_kernel(kinds, used, chunks, base, plan, *refs):
    count = len(kinds)
    blocks, refs = refs[: count * chunks], refs[count * chunks :]
    rights, refs = refs[: len(used) * chunks], refs[len(used) * chunks :]
    sums, out, full = refs[0], refs[-2], refs[-1]
    left = lax.broadcasted_iota(jnp.int32, (GROUP, 128), 1) < GROUP
    step = pl.program_id(0)

    for i, choices in enumerate(kinds):
        for kind in choices:

            @pl.when(plan[base + 2 * i] == kind)
            def _():
                mine = blocks[chunks * i : chunks * (i + 1)]
                turned = jnp.concatenate([block[...].T for block in mine], axis=0)
                ours = [rights[len(used) * c + used.index(kind)][...] for c in range(chunks)]
                value = jnp.dot(
                    turned, jnp.concatenate(ours, axis=1), preferred_element_type=jnp.float32
                )

                @pl.when(step == 0)
                def _():
                    full[i] = value

                @pl.when(step > 0)
                def _():
                    full[i] += value

    @pl.when(step == pl.num_programs(0) - 1)
    def _():
        out[...] = sums[...]
        for i in range(count):

            @pl.when(plan[base + 2 * i] < 3)
            def _():
                for other in range(chunks):
                    top = slice(128 * other, 128 * other + GROUP)
                    low = slice(128 * other + GROUP, 128 * (other + 1))
                    for m in range(2):
                        lanes = slice(128 * m, 128 * (m + 1))
                        value = full[i, top, lanes] + pltpu.roll(full[i, low, lanes], GROUP, 1)
                        if chunks == 2:
                            lanes = slice(256 + 128 * m, 256 + 128 * (m + 1))
                            second = pltpu.roll(full[i, top, lanes], GROUP, 1)
                            value = jnp.where(left, value, second + full[i, low, lanes])
                        out[m, plan[base + 2 * i + 1], other] += value


def gram(blocks, kinds, plan, base, rights, sums, limit, after=()):
    chunks = len(rights)
    steps = 3
    flat = [block.reshape(-1, 128) for block in blocks]
    used = sorted({kind for choices in kinds for kind in choices})
    right = [three[kind].reshape(-1, 256) for three in rights for kind in used]
    part = flat[0].shape[0] // steps
    whole = pl.BlockSpec(sums.shape, lambda s: (0,) * sums.ndim)
    return pl.pallas_call(
        functools.partial(gram_kernel, kinds, used, chunks, base),
        grid=(steps,),
        in_specs=[IN_SMEM]
        + [pl.BlockSpec((part, 128), lambda s: (s, 0))] * len(flat)
        + [pl.BlockSpec((part, 256), lambda s: (s, 0))] * len(right)
        + [whole]
        + [ANYWHERE] * len(after),
        out_specs=whole,
        out_shape=jax.ShapeDtypeStruct(sums.shape, jnp.float32),
        scratch_shapes=[pltpu.VMEM((len(kinds), 128 * chunks, 256 * chunks), jnp.float32)],
        compiler_params=pltpu.CompilerParams(vmem_limit_bytes=limit),
        cost_estimate=cost(len(flat) * flat[0].size * 8),
        name="gram",
    )(plan, *flat, *right, sums, *after)


def hop_operands(hop, up, down, low_a, low_b):
    bands = lax.axis_size("band")
    band = lax.axis_index("band")
    mid = bands // 2
    if hop == mid and mid > 1:
        up = jnp.where(band < mid - 1, low_b, up)
        down = jnp.where(band > bands - mid, low_a, down)
    return up, down


def behind(arrays, after):
    return pl.pallas_call(
        lambda *refs: None,
        in_specs=[ANYWHERE] * (len(arrays) + len(after)),
        out_specs=[ANYWHERE] * len(arrays),
        out_shape=[jax.ShapeDtypeStruct(x.shape, x.dtype) for x in arrays],
        input_output_aliases={i: i for i in range(len(arrays))},
        name="behind",
    )(*arrays, *after)


def hop_move(hop, up, down):
    bands = lax.axis_size("band")
    mid = bands // 2
    pairs = [b for b in range(hop, bands) if b - hop < mid]
    if hop >= mid:
        pairs = pairs + list(range(hop - mid + 1, mid))
    up = lax.ppermute(up, "band", [(b - 1, b) for b in pairs])
    down = lax.ppermute(down, "band", [(bands - b, bands - 1 - b) for b in pairs])
    return up, down


def hop_plan(hop, bands, band):
    mid = bands // 2
    late = hop - mid + 1
    skip = 3

    def one(place, main, other, sign):
        is_main = jnp.logical_and(place >= hop, place - hop < mid)
        is_late = jnp.logical_and(hop >= mid, jnp.logical_and(place >= late, place < mid))
        kind = jnp.where(is_main, main, jnp.where(is_late, other, skip))
        slot = band - sign * jnp.where(is_main, hop, jnp.where(is_late, late, 0))
        return [kind, slot]

    return one(band, 0, 1, 1) + one(bands - 1 - band, 2, 0, -1)


def summed_over_domain(table):
    count = lax.axis_size("domain")
    me = lax.axis_index("domain")
    table = table.reshape(2, count // 2, 2, table.shape[1] // count, table.shape[2])
    mine = lax.rem(me, 2)
    keep = lax.dynamic_index_in_dim(table, mine, axis=2, keepdims=False)
    send = lax.dynamic_index_in_dim(table, 1 - mine, axis=2, keepdims=False)
    table = keep + lax.ppermute(send, "domain", [(i, i ^ 1) for i in range(count)])
    total = lax.dynamic_index_in_dim(table, me // 2, axis=1, keepdims=False)
    for other in range(1, count // 2):
        send = lax.dynamic_index_in_dim(table, (me // 2) ^ other, axis=1, keepdims=False)
        pairs = [(i, i ^ (2 * other)) for i in range(count)]
        total = total + lax.ppermute(send, "domain", pairs)
    return total


def other_triangle(table):
    bands, count = lax.axis_size("band"), lax.axis_size("domain")
    d, b = lax.axis_index("domain"), lax.axis_index("band")
    ratio = count // bands
    rows = table.shape[1]
    place = lax.rem(d, ratio)
    pieces = []
    for shift in range(ratio):
        to = lax.rem(place + shift, ratio)
        block = lax.dynamic_slice_in_dim(table, to * rows, rows, axis=2)
        pairs = []
        for i in range(count):
            for j in range(bands):
                target = ratio * j + (i % ratio + shift) % ratio
                pairs.append((i * bands + j, target * bands + i // ratio))
        pieces.append(lax.ppermute(block, ("domain", "band"), pairs).transpose(0, 2, 1))
    ordered = [
        lax.dynamic_index_in_dim(
            jnp.stack(pieces), lax.rem(place - t + ratio, ratio), axis=0, keepdims=False
        )
        for t in range(ratio)
    ]
    out = jnp.concatenate(ordered, axis=2)
    return jnp.where(d // ratio == b, 0.0, out)


def pot_kernel(diagonal, out):
    flipped = halves(jnp.broadcast_to(diagonal[0], (GROUP, diagonal.shape[2])))
    for y in range(out.shape[1]):
        out[0, y] = flipped[y * NZ : (y + 1) * NZ]


def spread(diagonal):
    nx, cells = diagonal.shape
    ny = cells // NZ // 2
    return pl.pallas_call(
        pot_kernel,
        grid=(nx,),
        in_specs=[pl.BlockSpec((1, 1, cells), lambda s: (s, 0, 0))],
        out_specs=pl.BlockSpec((1, ny, NZ, 128), lambda s: (s, 0, 0, 0)),
        out_shape=jax.ShapeDtypeStruct((nx, ny, NZ, 128), jnp.float32),
        compiler_params=pltpu.CompilerParams(vmem_limit_bytes=SMALL_LIMIT),
        cost_estimate=cost(128 * nx * cells * 5),
        name="spread",
    )(diagonal.reshape(nx, 1, cells))


def shards(orbitals, potential):
    own, nx, cells = orbitals.shape
    chunks = own // GROUP
    bands = lax.axis_size("band")
    total_cells = lax.axis_size("domain") * potential.size

    pot = spread((3.0 * kinetic * coeffs[0] + potential - center) / half_width)

    field = orbitals.transpose(1, 0, 2)
    packed = [pack(field, c) for c in range(chunks)]
    cur = [packed[c][0] for c in range(chunks)]
    edges = [(packed[c][1], packed[c][2]) for c in range(chunks)]
    token = packed[-1][0]
    prev = [None] * chunks
    lows = [None] * chunks
    for step in range(4):
        mode = "first" if step == 0 else ("last" if step == 3 else "middle")
        for c in range(chunks):
            below, above = exchange(*edges[c])
            after = [token]
            earlier = edges[0] if step == 3 and c > 0 else ()
            out = apply_op(mode, cur[c], prev[c], below, above, pot, after=after, earlier=earlier)
            prev[c], cur[c], edges[c] = cur[c], out[0], (out[1], out[2])
            lows[c] = out[3:5]
            token = out[0]
    band = lax.axis_index("band")
    lower = (band < bands // 2).astype(jnp.int32).reshape(1)
    ups, downs = [[] for _ in range(chunks)], [[] for _ in range(chunks)]
    sending, rights = [], []

    def move(c, hop):
        up, down = hop_move(hop, *sending[c])
        ups[c].append(up)
        downs[c].append(down)

    for c in range(chunks):
        sending.append(tuple(lows[c]))
        move(c, 1)
    halo = exchange(*edges[-1])
    for c in range(chunks):
        if bands > 2:
            sending[c] = hop_operands(2, ups[c][0], downs[c][0], *lows[c])
            move(c, 2)
        after = [token] if c > 0 else [token, ups[0][-1], downs[0][-1]]
        chunk = c if chunks > 1 else None
        rights.append(apply_op("image", cur[c], None, *halo, pot, lower, after, chunk=chunk))
        token = rights[-1][0]
    zeros = jnp.zeros((2, bands, chunks, GROUP, 128), jnp.float32)
    for hop in range(3, bands):
        for c in range(chunks):
            sending[c] = hop_operands(hop, ups[c][-1], downs[c][-1], *lows[c])
            if hop == 3 and c == chunks - 1:
                ups[c][-1], downs[c][-1], zeros = behind([*sending[c], zeros], [token])
                sending[c] = (ups[c][-1], downs[c][-1])
            move(c, hop)

    plans = [hop_plan(hop, bands, band) for hop in range(1, bands)]
    late = [0 <= hop - bands // 2 < bands // 2 - 1 for hop in range(1, bands)]
    kinds = [((0, 1), (2, 0)) if behind else ((0,), (2,)) for behind in late]

    plan = [jnp.int32(0), band, jnp.int32(1), band]
    for one in plans:
        plan = plan + one
    plan = jnp.stack(plan).astype(jnp.int32)

    def add_products(sums, first, last, after=()):
        blocks, choice = [], []
        if first == 0:
            blocks = [lows[c][part] for part in range(2) for c in range(chunks)]
            choice = [(0,), (1,)]
        for i in range(max(first, 1) - 1, last):
            blocks += [ups[c][i] for c in range(chunks)] + [downs[c][i] for c in range(chunks)]
            choice += kinds[i]
        base = 4 * first
        limit = LAST_GRAM_LIMIT if last == bands - 1 else GRAM_LIMIT
        return gram(blocks, tuple(choice), plan, base, rights, sums, limit, after=after)

    done = max(bands - 2, 1)
    table = zeros
    for last in range(1, done + 1):
        table = add_products(table, 0 if last == 1 else last, last)
    filtered = unpack(cur, own, after=[table])
    if bands > done + 1:
        table = add_products(table, bands - 1, bands - 1, [filtered])
    table = table.reshape(2, bands * own, 128)[:, :, :own]
    table = summed_over_domain(table)
    table = (table + other_triangle(table)) / total_cells
    return (filtered.transpose(1, 0, 2), table[0], table[1])


def solution(mesh):
    placed = (P("band", "domain", None), P("domain", None))
    return jax.shard_map(
        shards,
        mesh=mesh,
        in_specs=placed,
        out_specs=(P("band", "domain", None), P("domain", "band"), P("domain", "band")),
        check_vma=False,
    )
```
